32 devices in a mesh: seq: 8 (over z, x), head: 4 (over y, core).
Axes of the slice: x: 2, y: 2, z: 4, core: 2. Of those that a mesh axis runs over, the one named last changes fastest.
Arguments:
- queries: bfloat16 [2048, 2048], P('seq', 'head'), may hold values from -6 to 6
- keys: bfloat16 [2048, 2048], P('seq', 'head'), may hold values from -6 to 6
- values: bfloat16 [2048, 2048], P('seq', 'head'), may hold values from -6 to 6
- out_grad: bfloat16 [2048, 2048], P(('seq', 'head')), may hold values from -6 to 6
Outputs:
- attended: bfloat16 [2048, 2048], P('seq', 'head')
- query_grad: bfloat16 [2048, 2048], P('seq', 'head')
- key_grad: bfloat16 [2048, 2048], P('seq', 'head')
- value_grad: bfloat16 [2048, 2048], P('seq', 'head')
The draws below stay inside these ranges and needn't reach their ends.
All inputs are finite; a program needn't handle non-finite values.
Results may differ from the reference program's by a relative error of at most 0.0049.
Values may be sent and summed in bfloat16 or wider, within the bound.
No kernel may reach another device: no remote copies, remote signals or barrier semaphores. Data moves between devices by JAX's collectives and lax.ppermute only.
A program may use at most 64 MiB of HBM per device.

```python
import math
import jax
import jax.numpy as jnp
from jax import lax

H = 32
DH = 64
BLOCK = 256
TOKENS = 2048


def steps_of(own_key, extent, pieces, least, largest):
    gain = 1.0
    for axis_at, shards_of in pieces:
        draws = jax.random.uniform(jax.random.fold_in(jax.random.fold_in(own_key, 6), axis_at), (shards_of,), jnp.float32, least / len(pieces), largest / len(pieces))
        gain = gain * jnp.repeat(jnp.exp(draws), extent[axis_at] // shards_of).reshape((-1,) + (1,) * (len(extent) - 1 - axis_at))
    return gain


def normal_values(rng, shape, width, most, cuts=(), kind=jnp.bfloat16):
    level = steps_of(rng, shape, cuts, -0.22, 0.18) if cuts else 1.0
    drawn = jax.random.normal(rng, shape, jnp.float32) * width * level
    return jnp.minimum(jnp.maximum(drawn, -most), most).astype(kind)


def setup_inputs(seed: int = 0) -> dict:
    arg_keys = jax.random.split(jax.random.key(seed), 5)
    return {
        "queries": normal_values(arg_keys[0], (TOKENS, H * DH), 1.0, 6.0, ((0, 8), (1, 4))),
        "keys": normal_values(arg_keys[1], (TOKENS, H * DH), 1.0, 6.0, ((0, 8), (1, 4))),
        "values": normal_values(arg_keys[2], (TOKENS, H * DH), 1.0, 6.0, ((0, 8), (1, 4))),
        "out_grad": normal_values(arg_keys[3], (TOKENS, H * DH), 1.0, 6.0, ((0, 32),)),
    }


def round_back(array):
    return lax.optimization_barrier(array.astype(jnp.bfloat16)).astype(jnp.float32)

def head_pass(parts):
    q_head, k_head, v_head, g_head = parts
    q_full = q_head.astype(jnp.float32)
    k_full = k_head.astype(jnp.float32)
    v_full = v_head.astype(jnp.float32)
    g_full = g_head.astype(jnp.float32)
    factor = 1.0 / math.sqrt(DH * TOKENS)
    causal = jnp.arange(BLOCK)[:, None] >= jnp.arange(BLOCK)[None, :]
    block_state = jnp.einsum('nta,ntb->nab', k_full, v_full)
    prefix_state = round_back(jnp.cumsum(block_state, 0) - block_state)
    grad_state = jnp.einsum('nta,ntb->nab', q_full, g_full)
    suffix_state = round_back(jnp.cumsum(grad_state[::-1], 0)[::-1] - grad_state)
    scores = jnp.einsum('nia,nja->nij', q_full, k_full) * factor
    probs = round_back(jnp.where(causal[None], scores, 0.0))
    attended = jnp.einsum('nij,njb->nib', probs, v_full) + factor * jnp.einsum('nia,nab->nib', q_full, prefix_state)
    dscores = jnp.einsum('nib,njb->nij', g_full, v_full) * factor
    dprobs = round_back(jnp.where(causal[None], dscores, 0.0))
    query_grad = jnp.einsum('nij,nja->nia', dprobs, k_full) + factor * jnp.einsum('nib,nab->nia', g_full, prefix_state)
    key_grad = jnp.einsum('nij,nia->nja', dprobs, q_full) + factor * jnp.einsum('njb,nab->nja', v_full, suffix_state)
    value_grad = jnp.einsum('nij,nib->njb', probs, g_full) + factor * jnp.einsum('nja,nab->njb', k_full, suffix_state)
    return (attended.astype(jnp.bfloat16), query_grad.astype(jnp.bfloat16), key_grad.astype(jnp.bfloat16), value_grad.astype(jnp.bfloat16))

def split_heads(array):
    blocks = TOKENS // BLOCK
    return array.reshape(blocks, BLOCK, H, DH).transpose(2, 0, 1, 3)

def join_heads(array):
    return array.transpose(1, 2, 0, 3).reshape(TOKENS, H * DH)

def reference(queries, keys, values, out_grad):
    results = lax.map(head_pass, (split_heads(queries), split_heads(keys), split_heads(values), split_heads(out_grad)))
    return (join_heads(results[0]), join_heads(results[1]), join_heads(results[2]), join_heads(results[3]))
```

```python
import functools
import math

import jax
import jax.numpy as jnp
from jax import lax
from jax.experimental import pallas as pl
from jax.experimental.pallas import tpu as pltpu
from jax.sharding import PartitionSpec as P

DH = 64
BLOCK = 256
PAIR = 2 * DH
VMEM = pl.BlockSpec(memory_space=pltpu.VMEM)
SMEM = pl.BlockSpec(memory_space=pltpu.SMEM)


def dot(a, b, dims):
    return lax.dot_general(a, b, ((dims[:1], dims[1:]), ((), ())), preferred_element_type=jnp.float32)


def first_half(shape):
    return lax.broadcasted_iota(jnp.int32, shape, len(shape) - 1) < DH


def split_pair(x):
    mask = first_half(x.shape)
    zero = jnp.zeros_like(x)
    return jnp.where(mask, x, zero), jnp.where(mask, zero, x)


def pair_state(a, b):
    whole = dot(a, b, (0, 0))
    return jnp.where(first_half((DH, PAIR)), whole[:DH], whole[DH:])


def spread_state(state):
    return jnp.concatenate(split_pair(state), axis=0)


def masked(scores, factor, upper):
    row = lax.broadcasted_iota(jnp.int32, scores.shape, 0)
    col = lax.broadcasted_iota(jnp.int32, scores.shape, 1)
    keep = col >= row if upper else col <= row
    return jnp.where(keep, scores * factor, 0.0).astype(jnp.bfloat16)


def pair_columns(p):
    return slice(p * PAIR, (p + 1) * PAIR)


def state_rows(p):
    return slice(p * DH, (p + 1) * DH)


def block_rows(n):
    return slice(n * BLOCK, (n + 1) * BLOCK)


def state_kernel(a_ref, b_ref, out_ref):
    pairs = a_ref.shape[1] // PAIR
    for n in range(a_ref.shape[0] // BLOCK):
        for p in range(pairs):
            a = a_ref[block_rows(n), pair_columns(p)]
            b = b_ref[block_rows(n), pair_columns(p)]
            out_ref[n, state_rows(p), :] = pair_state(a, b)


def gather_kernel(head_ref, q_ref, g_ref, *refs):
    pieces, (grad_ref, out_ref) = refs[:-2], refs[-2:]
    me = head_ref[0]
    rows, width = g_ref.shape[0], q_ref.shape[1]
    count = len(pieces) + 1
    own = g_ref[:, pl.ds(pl.multiple_of(me * width, width), width)]
    grad_ref[pl.ds(pl.multiple_of(me * rows, rows), rows), :] = own
    for d, piece in enumerate(pieces, 1):
        source = partner(me, d, count)
        grad_ref[pl.ds(pl.multiple_of(source * rows, rows), rows), :] = piece[...]
    state_kernel(q_ref, grad_ref, out_ref)


def forward_kernel(factor, q_ref, k_ref, v_ref, att_ref):
    for n in range(q_ref.shape[0] // BLOCK):
        for p in range(q_ref.shape[1] // PAIR):
            at = (block_rows(n), pair_columns(p))
            q, k, v = q_ref[at], k_ref[at], v_ref[at]
            total = 0.0
            for q_head, v_head in zip(split_pair(q), split_pair(v)):
                probs = masked(dot(q_head, k, (1, 1)), factor, False)
                total = total + dot(probs, v_head, (1, 0))
            att_ref[at] = total


def backward_kernel(factor, q_ref, k_ref, v_ref, g_ref, dq_ref, dk_ref, dv_ref):
    for n in range(q_ref.shape[0] // BLOCK):
        for p in range(q_ref.shape[1] // PAIR):
            at = (block_rows(n), pair_columns(p))
            q, k, v, g = q_ref[at], k_ref[at], v_ref[at], g_ref[at]
            dq = dk = dv = 0.0
            for q_head, k_head, v_head, g_head in zip(*map(split_pair, (q, k, v, g))):
                probs_t = masked(dot(k_head, q, (1, 1)), factor, True)
                dv = dv + dot(probs_t, g_head, (1, 0))
                dprobs = masked(dot(g_head, v, (1, 1)), factor, False)
                dq = dq + dot(dprobs, k_head, (1, 0))
                dprobs_t = masked(dot(v_head, g, (1, 1)), factor, True)
                dk = dk + dot(dprobs_t, q_head, (1, 0))
            dq_ref[at] = dq
            dk_ref[at] = dk
            dv_ref[at] = dv


def join_kernel(factor, a_ref, b_ref, state_ref, a_part_ref, b_part_ref, a_out_ref, b_out_ref):
    for n in range(a_ref.shape[0] // BLOCK):
        for p in range(a_ref.shape[1] // PAIR):
            at = (block_rows(n), pair_columns(p))
            state = spread_state(state_ref[n, state_rows(p), :])
            a_out_ref[at] = (a_part_ref[at] + factor * dot(a_ref[at], state, (1, 0))).astype(jnp.bfloat16)
            b_out_ref[at] = (b_part_ref[at] + factor * dot(b_ref[at], state, (1, 1))).astype(jnp.bfloat16)


def partner(index, d, count):
    if count & (count - 1) == 0:
        return index ^ d
    return lax.rem(index - d + count, count)


def call(kernel, out_shapes, operands, flops, scalars=0):
    out_bytes = sum(math.prod(s.shape) * s.dtype.itemsize for s in out_shapes)
    in_bytes = sum(math.prod(x.shape) * x.dtype.itemsize for x in operands)
    single = len(out_shapes) == 1
    return pl.pallas_call(
        kernel,
        out_shape=out_shapes[0] if single else out_shapes,
        in_specs=[SMEM] * scalars + [VMEM] * (len(operands) - scalars),
        out_specs=VMEM if single else [VMEM] * len(out_shapes),
        compiler_params=pltpu.CompilerParams(vmem_limit_bytes=24 * 1024 * 1024),
        cost_estimate=pl.CostEstimate(flops=flops, bytes_accessed=in_bytes + out_bytes, transcendentals=0),
    )(*operands)


def out_grad_pieces(out_grad, width):
    count = lax.axis_size("head")
    me = lax.axis_index("head")
    pieces = []
    for d in range(1, count):
        if count & (count - 1) == 0:
            target = me ^ d
            pairs = [(i, i ^ d) for i in range(count)]
        else:
            target = lax.rem(me + d, count)
            pairs = [(i, (i + d) % count) for i in range(count)]
        block = lax.dynamic_slice_in_dim(out_grad, target * width, width, 1)
        pieces.append(lax.ppermute(block, "head", pairs))
    return pieces


def scan_over_seq(own, later):
    count = lax.axis_size("seq")
    me = lax.axis_index("seq")
    total = own
    found = jnp.zeros_like(own)
    span = 1
    while span < count:
        if count & (count - 1) == 0:
            pairs = [(i, i ^ span) for i in range(count)]
            got = lax.ppermute(total.astype(jnp.bfloat16), "seq", pairs).astype(jnp.float32)
            beyond = (me & span == 0) if later else (me & span != 0)
            found = found + jnp.where(beyond, got, 0.0)
            total = total + got
        else:
            step = -span if later else span
            pairs = [(i, i + step) for i in range(count) if 0 <= i + step < count]
            got = lax.ppermute(total.astype(jnp.bfloat16), "seq", pairs).astype(jnp.float32)
            found = found + got
            total = total + got
        span *= 2
    return found


def within(blocks, later):
    if blocks.shape[0] == 1:
        return jnp.zeros_like(blocks)
    if later:
        return jnp.cumsum(blocks[::-1], 0)[::-1] - blocks
    return jnp.cumsum(blocks, 0) - blocks


def on_device(queries, keys, values, out_grad):
    rows, width = queries.shape
    pairs, blocks = width // PAIR, rows // BLOCK
    factor = 1.0 / math.sqrt(DH * rows * lax.axis_size("seq"))
    product = 2 * rows * BLOCK * width
    state_flops = 2 * rows * DH * width
    states = jax.ShapeDtypeStruct((blocks, pairs * DH, PAIR), jnp.float32)
    part = jax.ShapeDtypeStruct((rows, width), jnp.float32)
    whole = jax.ShapeDtypeStruct((rows, width), jnp.bfloat16)

    pieces = out_grad_pieces(out_grad, width)
    block_state = call(state_kernel, [states], (keys, values), state_flops)
    before = scan_over_seq(jnp.sum(block_state, 0), False)
    prefix_state = (before[None] + within(block_state, False)).astype(jnp.bfloat16)
    attended_part = call(
        functools.partial(forward_kernel, factor), [part], (queries, keys, values), 2 * product
    )
    head = lax.axis_index("head").astype(jnp.int32).reshape(1)
    grad, grad_state = call(
        gather_kernel, [whole, states], (head, queries, out_grad, *pieces), state_flops, scalars=1
    )
    after = scan_over_seq(jnp.sum(grad_state, 0), True)
    suffix_state = (after[None] + within(grad_state, True)).astype(jnp.bfloat16)
    query_part, key_part, value_part = call(
        functools.partial(backward_kernel, factor),
        [part, part, part],
        (queries, keys, values, grad),
        6 * product,
    )
    join = functools.partial(join_kernel, factor)
    attended, query_grad = call(
        join, [whole, whole], (queries, grad, prefix_state, attended_part, query_part), 2 * state_flops
    )
    value_grad, key_grad = call(
        join, [whole, whole], (keys, values, suffix_state, value_part, key_part), 2 * state_flops
    )
    return attended, query_grad, key_grad, value_grad


def solution(mesh):
    split = P("seq", "head")
    return jax.shard_map(
        on_device,
        mesh=mesh,
        in_specs=(split, split, split, P(("seq", "head"), None)),
        out_specs=(split, split, split, split),
        check_vma=False,
    )
```

```python
import functools
import math

import jax
import jax.numpy as jnp
from jax import lax
from jax.experimental import pallas as pl
from jax.experimental.pallas import tpu as pltpu
from jax.sharding import PartitionSpec as P

DH = 64
BLOCK = 256
PAIR = 2 * DH
VMEM = pl.BlockSpec(memory_space=pltpu.VMEM)
SMEM = pl.BlockSpec(memory_space=pltpu.SMEM)
HBM = pl.BlockSpec(memory_space=pltpu.HBM)
ANY = pl.BlockSpec(memory_space=pl.ANY)


def dot(a, b, dims):
    return lax.dot_general(a, b, ((dims[:1], dims[1:]), ((), ())), preferred_element_type=jnp.float32)


def first_half(shape):
    return lax.broadcasted_iota(jnp.int32, shape, len(shape) - 1) < DH


def split_pair(x):
    mask = first_half(x.shape)
    zero = jnp.zeros_like(x)
    return jnp.where(mask, x, zero), jnp.where(mask, zero, x)


def pair_state(a, b):
    whole = dot(a, b, (0, 0))
    return jnp.where(first_half((DH, PAIR)), whole[:DH], whole[DH:])


def spread_state(state):
    return jnp.concatenate(split_pair(state), axis=0)


def masked(scores, factor, upper):
    row = lax.broadcasted_iota(jnp.int32, scores.shape, 0)
    col = lax.broadcasted_iota(jnp.int32, scores.shape, 1)
    keep = col >= row if upper else col <= row
    return jnp.where(keep, scores * factor, 0.0).astype(jnp.bfloat16)


def pair_columns(p):
    return slice(p * PAIR, (p + 1) * PAIR)


def state_rows(p):
    return slice(p * DH, (p + 1) * DH)


def block_rows(n):
    return slice(n * BLOCK, (n + 1) * BLOCK)


def state_kernel(a_ref, b_ref, out_ref):
    pairs = a_ref.shape[1] // PAIR
    for n in range(a_ref.shape[0] // BLOCK):
        for p in range(pairs):
            a = a_ref[block_rows(n), pair_columns(p)]
            b = b_ref[block_rows(n), pair_columns(p)]
            out_ref[n, state_rows(p), :] = pair_state(a, b)


def prepare_kernel(head_ref, g_ref, v_ref, *refs):
    pieces, v_out_ref, sems = refs[:-2], refs[-2], refs[-1]
    width, count = v_ref.shape[1], len(pieces)
    copies = []
    for d, piece in enumerate(pieces):
        columns = pl.ds(pl.multiple_of(receiver(head_ref[0], d, count) * width, width), width)
        copies.append(pltpu.make_async_copy(g_ref.at[:, columns], piece, sems.at[d]))
    copies.append(pltpu.make_async_copy(v_ref, v_out_ref, sems.at[count]))
    for copy in copies:
        copy.start()
    for copy in copies:
        copy.wait()


def gather_kernel(head_ref, q_ref, *refs):
    pieces, (grad_ref, out_ref) = refs[:-2], refs[-2:]
    rows, count = pieces[0].shape[0], len(pieces)
    for d, piece in enumerate(pieces):
        source = sender(head_ref[0], d, count)
        grad_ref[pl.ds(pl.multiple_of(source * rows, rows), rows), :] = piece[...]
    state_kernel(q_ref, grad_ref, out_ref)


def forward_kernel(factor, q_ref, k_ref, v_ref, _, att_ref):
    for n in range(q_ref.shape[0] // BLOCK):
        for p in range(q_ref.shape[1] // PAIR):
            at = (block_rows(n), pair_columns(p))
            q, k, v = q_ref[at], k_ref[at], v_ref[at]
            total = 0.0
            for q_head, v_head in zip(split_pair(q), split_pair(v)):
                probs = masked(dot(q_head, k, (1, 1)), factor, False)
                total = total + dot(probs, v_head, (1, 0))
            att_ref[at] = total


def backward_kernel(factor, q_ref, k_ref, v_ref, g_ref, _, dq_ref, dk_ref, dv_ref):
    for n in range(q_ref.shape[0] // BLOCK):
        for p in range(q_ref.shape[1] // PAIR):
            at = (block_rows(n), pair_columns(p))
            q, k, v, g = q_ref[at], k_ref[at], v_ref[at], g_ref[at]
            dq = dk = dv = 0.0
            for q_head, k_head, v_head, g_head in zip(*map(split_pair, (q, k, v, g))):
                probs_t = masked(dot(k_head, q, (1, 1)), factor, True)
                dv = dv + dot(probs_t, g_head, (1, 0))
                dprobs = masked(dot(g_head, v, (1, 1)), factor, False)
                dq = dq + dot(dprobs, k_head, (1, 0))
                dprobs_t = masked(dot(v_head, g, (1, 1)), factor, True)
                dk = dk + dot(dprobs_t, q_head, (1, 0))
            dq_ref[at] = dq
            dk_ref[at] = dk
            dv_ref[at] = dv


def join(factor, state_ref, a, b):
    copies = []
    for n in range(a[0].shape[0] // BLOCK):
        for p in range(a[0].shape[1] // PAIR):
            at = (block_rows(n), pair_columns(p))
            state = spread_state(state_ref[n, state_rows(p), :])
            for (x_ref, part_ref, held, out_ref, sems), side in ((a, 0), (b, 1)):
                added = factor * dot(x_ref[at], state, (1, side))
                held[at] = (part_ref[at] + added).astype(jnp.bfloat16)
                copy = pltpu.make_async_copy(held.at[at], out_ref.at[at], sems.at[n, p])
                copy.start()
                copies.append(copy)
    for copy in copies:
        copy.wait()


def join_kernel(factor, forward, forward_ref, state_ref, q_ref, k_ref, v_ref, g_ref, att_part, dq_part, dk_part, dv_part, *refs):
    att_ref, dq_ref, dk_ref, dv_ref, a_held, b_held, a_sems, b_sems = refs[-8:]
    is_forward = forward_ref[0] == int(forward)

    @pl.when(is_forward)
    def _():
        a = (q_ref, att_part, a_held, att_ref, a_sems)
        b = (g_ref, dq_part, b_held, dq_ref, b_sems)
        join(factor, state_ref, a, b)

    @pl.when(jnp.logical_not(is_forward))
    def _():
        a = (k_ref, dv_part, a_held, dv_ref, a_sems)
        b = (v_ref, dk_part, b_held, dk_ref, b_sems)
        join(factor, state_ref, a, b)


def in_pairs(count):
    return count & (count - 1) == 0


def receiver(index, d, count):
    return index ^ d if in_pairs(count) else lax.rem(index + d, count)


def sender(index, d, count):
    return index ^ d if in_pairs(count) else lax.rem(index - d + count, count)


def exchange(x, axis, d):
    count = lax.axis_size(axis)
    return lax.ppermute(x, axis, [(i, i ^ d if in_pairs(count) else (i + d) % count) for i in range(count)])


def passed_along(x, axis, step):
    count = lax.axis_size(axis)
    return lax.ppermute(x, axis, [(i, i + step) for i in range(count) if 0 <= i + step < count])


def call(kernel, out_shapes, operands, microseconds, out_specs=None, in_specs=None, **options):
    return pl.pallas_call(
        kernel,
        out_shape=out_shapes,
        in_specs=in_specs or [VMEM] * len(operands),
        out_specs=out_specs or [VMEM] * len(out_shapes),
        compiler_params=pltpu.CompilerParams(vmem_limit_bytes=24 * 1024 * 1024),
        cost_estimate=pl.CostEstimate(flops=int(1.15e9 * microseconds), bytes_accessed=0, transcendentals=0),
        **options,
    )(*operands)


def wire(x):
    return x.astype(jnp.bfloat16)


def wide(x):
    return x.astype(jnp.float32)


class Scan:
    def __init__(self, own, later):
        self.total, self.found, self.later, self.span = own, jnp.zeros_like(own), later, 1

    def step(self):
        count, me = lax.axis_size("seq"), lax.axis_index("seq")
        if in_pairs(count):
            got = wide(exchange(wire(self.total), "seq", self.span))
            beyond = (me & self.span == 0) if self.later else (me & self.span != 0)
            self.found = self.found + jnp.where(beyond, got, 0.0)
        else:
            got = wide(passed_along(wire(self.total), "seq", -self.span if self.later else self.span))
            self.found = self.found + got
        self.total = self.total + got
        self.span *= 2
        return got


def within(blocks, later):
    if blocks.shape[0] == 1:
        return jnp.zeros_like(blocks)
    if later:
        return jnp.cumsum(blocks[::-1], 0)[::-1] - blocks
    return jnp.cumsum(blocks, 0) - blocks


def on_device(queries, keys, values, out_grad):
    rows, width = queries.shape
    pairs, blocks = width // PAIR, rows // BLOCK
    factor = 1.0 / math.sqrt(DH * rows * lax.axis_size("seq"))
    states = jax.ShapeDtypeStruct((blocks, pairs * DH, PAIR), jnp.float32)
    part = jax.ShapeDtypeStruct((rows, width), jnp.float32)
    whole = jax.ShapeDtypeStruct((rows, width), jnp.bfloat16)
    piece = jax.ShapeDtypeStruct((out_grad.shape[0], width), jnp.bfloat16)
    heads, seqs = lax.axis_size("head"), lax.axis_size("seq")
    head = lax.axis_index("head").astype(jnp.int32).reshape(1)

    *pieces, held_values = call(
        prepare_kernel,
        [piece] * heads + [whole],
        (head, pltpu.with_memory_space_constraint(out_grad, pltpu.HBM), pltpu.with_memory_space_constraint(values, pltpu.HBM)),
        1.2,
        in_specs=[SMEM, HBM, HBM],
        scratch_shapes=[pltpu.SemaphoreType.DMA((heads + 1,))],
    )
    pieces = [pieces[0]] + [exchange(pieces[d], "head", d) for d in range(1, heads)]
    (block_state,) = call(state_kernel, [states], (keys, held_values), 0.3)
    before = Scan(jnp.sum(block_state, 0), False)
    before.step()
    grad, grad_state = call(
        gather_kernel,
        [whole, states],
        (head, queries, *pieces),
        0.3,
        in_specs=[SMEM] + [VMEM] * (heads + 1),
    )
    after = Scan(jnp.sum(grad_state, 0), True)
    got = after.step()
    (attended_part,) = call(
        functools.partial(forward_kernel, factor),
        [part],
        (queries, keys, held_values, grad_state),
        1.0,
        in_specs=[VMEM] * 3 + [ANY],
    )
    parts = call(
        functools.partial(backward_kernel, factor),
        [part, part, part],
        (queries, keys, held_values, grad, got),
        2.5,
        in_specs=[VMEM] * 4 + [ANY],
    )
    last = seqs // 2 if in_pairs(seqs) else seqs
    while before.span < last:
        before.step()
        after.step()
    prefix = before.found[None] + within(block_state, False)
    suffix = after.found[None] + within(grad_state, True)
    if in_pairs(seqs) and seqs > 1:
        lower = lax.axis_index("seq") & last == 0
        rest = wide(exchange(wire(jnp.where(lower, before.total, after.total)), "seq", last))
        early, late = jnp.where(lower, prefix, suffix), jnp.where(lower, suffix, prefix) + rest[None]
    else:
        lower = lax.axis_index("seq") >= 0
        early, late = prefix, suffix
    flag = lower.astype(jnp.int32).reshape(1)
    operands = (queries, keys, held_values, grad, attended_part, *parts)
    results = ()
    for forward, state in ((True, early), (False, late)):
        results = call(
            functools.partial(join_kernel, factor, forward),
            [whole] * 4,
            (flag, wire(state), *operands, *results),
            1.0,
            in_specs=[SMEM] + [VMEM] * 9 + [HBM] * len(results),
            out_specs=[HBM] * 4,
            scratch_shapes=[pltpu.VMEM((rows, width), jnp.bfloat16)] * 2
            + [pltpu.SemaphoreType.DMA((blocks, pairs))] * 2,
            input_output_aliases={10 + i: i for i in range(len(results))},
        )
    return tuple(results)


def solution(mesh):
    split = P("seq", "head")
    return jax.shard_map(
        on_device,
        mesh=mesh,
        in_specs=(split, split, split, P(("seq", "head"), None)),
        out_specs=(split, split, split, split),
        check_vma=False,
    )
```

```python
import functools
import math

import jax
import jax.numpy as jnp
from jax import lax
from jax.experimental import pallas as pl
from jax.experimental.pallas import tpu as pltpu
from jax.sharding import PartitionSpec as P

DH = 64
BLOCK = 256
PAIR = 2 * DH
VMEM = pl.BlockSpec(memory_space=pltpu.VMEM)
SMEM = pl.BlockSpec(memory_space=pltpu.SMEM)
HBM = pl.BlockSpec(memory_space=pltpu.HBM)
ANY = pl.BlockSpec(memory_space=pl.ANY)


def dot(a, b, dims):
    return lax.dot_general(a, b, ((dims[:1], dims[1:]), ((), ())), preferred_element_type=jnp.float32)


def first_half(shape):
    return lax.broadcasted_iota(jnp.int32, shape, len(shape) - 1) < DH


def split_pair(x):
    mask = first_half(x.shape)
    zero = jnp.zeros_like(x)
    return jnp.where(mask, x, zero), jnp.where(mask, zero, x)


def pair_state(a, b):
    whole = dot(a, b, (0, 0))
    return jnp.where(first_half((DH, PAIR)), whole[:DH], whole[DH:])


def spread_state(state):
    return jnp.concatenate(split_pair(state), axis=0)


def masked(scores, factor, upper):
    row = lax.broadcasted_iota(jnp.int32, scores.shape, 0)
    col = lax.broadcasted_iota(jnp.int32, scores.shape, 1)
    keep = col >= row if upper else col <= row
    return jnp.where(keep, scores * factor, 0.0).astype(jnp.bfloat16)


def pair_columns(p):
    return slice(p * PAIR, (p + 1) * PAIR)


def state_rows(p):
    return slice(p * DH, (p + 1) * DH)


def block_rows(n):
    return slice(n * BLOCK, (n + 1) * BLOCK)


def state_kernel(a_ref, b_ref, out_ref, wire_ref):
    for p in range(a_ref.shape[1] // PAIR):
        total = 0.0
        for n in range(a_ref.shape[0] // BLOCK):
            state = pair_state(a_ref[block_rows(n), pair_columns(p)], b_ref[block_rows(n), pair_columns(p)])
            out_ref[n, state_rows(p), :] = state
            total = total + state
        wire_ref[state_rows(p), :] = wire(total)


def prepare_kernel(head_ref, g_ref, *refs):
    pieces, sems = refs[:-1], refs[-1]
    width, count = pieces[0].shape[1], len(pieces) + 2
    copies = []
    for d, piece in enumerate(pieces, 2):
        columns = pl.ds(pl.multiple_of(receiver(head_ref[0], d, count) * width, width), width)
        copies.append(pltpu.make_async_copy(g_ref.at[:, columns], piece, sems.at[d - 2]))
    for copy in copies:
        copy.start()
    for copy in copies:
        copy.wait()


def gather_kernel(head_ref, q_ref, g_ref, first_ref, *refs):
    pieces, (_, grad_ref, out_ref, wire_ref) = refs[:-4], refs[-4:]
    rows, width, count = g_ref.shape[0], q_ref.shape[1], len(pieces) + 2
    columns = pl.ds(pl.multiple_of(head_ref[0] * width, width), width)
    pieces = (g_ref.at[:, columns], first_ref.at[:, columns], *pieces)
    for d, piece in enumerate(pieces):
        source = sender(head_ref[0], d, count)
        grad_ref[pl.ds(pl.multiple_of(source * rows, rows), rows), :] = piece[...]
    state_kernel(q_ref, grad_ref, out_ref, wire_ref)


def forward_kernel(factor, q_ref, k_ref, v_ref, att_ref):
    for n in range(q_ref.shape[0] // BLOCK):
        for p in range(q_ref.shape[1] // PAIR):
            at = (block_rows(n), pair_columns(p))
            q, k, v = q_ref[at], k_ref[at], v_ref[at]
            total = 0.0
            for q_head, v_head in zip(split_pair(q), split_pair(v)):
                probs = masked(dot(q_head, k, (1, 1)), factor, False)
                total = total + dot(probs, v_head, (1, 0))
            att_ref[at] = total


def query_grad_kernel(factor, turn, turn_ref, k_ref, v_ref, g_ref, *refs):
    dq_ref = refs[-1]

    pairs = k_ref.shape[1] // PAIR

    @pl.when(turn_ref[0] == turn)
    def _():
        query_grad(factor, k_ref, v_ref, g_ref, dq_ref, range(pairs // 2))

    if turn == 0:
        query_grad(factor, k_ref, v_ref, g_ref, dq_ref, range(pairs // 2, pairs))


def query_grad(factor, k_ref, v_ref, g_ref, dq_ref, some):
    for n in range(k_ref.shape[0] // BLOCK):
        for p in some:
            at = (block_rows(n), pair_columns(p))
            k, v, g = k_ref[at], v_ref[at], g_ref[at]
            total = 0.0
            for k_head, g_head in zip(split_pair(k), split_pair(g)):
                dprobs = masked(dot(g_head, v, (1, 1)), factor, False)
                total = total + dot(dprobs, k_head, (1, 0))
            dq_ref[at] = total


def key_value_grad_kernel(factor, q_ref, k_ref, v_ref, g_ref, dk_ref, dv_ref):
    for n in range(q_ref.shape[0] // BLOCK):
        for p in range(q_ref.shape[1] // PAIR):
            at = (block_rows(n), pair_columns(p))
            q, k, v, g = q_ref[at], k_ref[at], v_ref[at], g_ref[at]
            dk = dv = 0.0
            for q_head, k_head, v_head, g_head in zip(*map(split_pair, (q, k, v, g))):
                probs_t = masked(dot(k_head, q, (1, 1)), factor, True)
                dv = dv + dot(probs_t, g_head, (1, 0))
                dprobs_t = masked(dot(v_head, g, (1, 1)), factor, True)
                dk = dk + dot(dprobs_t, q_head, (1, 0))
            dk_ref[at] = dk
            dv_ref[at] = dv


def join(factor, state_of, a, b):
    copies = []
    for n in range(a[0].shape[0] // BLOCK):
        for p in range(a[0].shape[1] // PAIR):
            at = (block_rows(n), pair_columns(p))
            state = spread_state(state_of(n, state_rows(p)))
            for (x_ref, part_ref, held, out_ref, sems), side in ((a, 0), (b, 1)):
                added = factor * dot(x_ref[at], state, (1, side))
                held[at] = (part_ref[at] + added).astype(jnp.bfloat16)
                copy = pltpu.make_async_copy(held.at[at], out_ref.at[at], sems.at[n, p])
                copy.start()
                copies.append(copy)
    for copy in copies:
        copy.wait()


def join_kernel(factor, forward, takes, flags_ref, base_ref, *refs):
    got_refs, refs = refs[:takes], refs[takes:]
    q_ref, k_ref, v_ref, g_ref, att_part, dq_part, dk_part, dv_part = refs[:8]
    att_ref, dq_ref, dk_ref, dv_ref, a_held, b_held, a_sems, b_sems = refs[-8:]
    is_forward = flags_ref[0] & 1 == int(forward)

    def state_of(n, rows):
        state = base_ref[n, rows, :]
        for i, got_ref in enumerate(got_refs, 1):
            state = state + jnp.where(flags_ref[0] >> i & 1 == 1, wide(got_ref[rows, :]), 0.0)
        return wire(state)

    @pl.when(is_forward)
    def _():
        a = (q_ref, att_part, a_held, att_ref, a_sems)
        b = (g_ref, dq_part, b_held, dq_ref, b_sems)
        join(factor, state_of, a, b)

    @pl.when(jnp.logical_not(is_forward))
    def _():
        a = (k_ref, dv_part, a_held, dv_ref, a_sems)
        b = (v_ref, dk_part, b_held, dk_ref, b_sems)
        join(factor, state_of, a, b)


def in_pairs(count):
    return count & (count - 1) == 0


def receiver(index, d, count):
    return index ^ d if in_pairs(count) else lax.rem(index + d, count)


def sender(index, d, count):
    return index ^ d if in_pairs(count) else lax.rem(index - d + count, count)


def exchange(x, axis, d):
    count = lax.axis_size(axis)
    return lax.ppermute(x, axis, [(i, i ^ d if in_pairs(count) else (i + d) % count) for i in range(count)])


def passed_along(x, axis, step):
    count = lax.axis_size(axis)
    return lax.ppermute(x, axis, [(i, i + step) for i in range(count) if 0 <= i + step < count])


def call(kernel, out_shapes, operands, microseconds, out_specs=None, in_specs=None, **options):
    return pl.pallas_call(
        kernel,
        out_shape=out_shapes,
        in_specs=in_specs or [VMEM] * len(operands),
        out_specs=out_specs or [VMEM] * len(out_shapes),
        compiler_params=pltpu.CompilerParams(vmem_limit_bytes=24 * 1024 * 1024),
        cost_estimate=pl.CostEstimate(flops=int(1.15e9 * microseconds), bytes_accessed=0, transcendentals=0),
        **options,
    )(*operands)


def wire(x):
    return x.astype(jnp.bfloat16)


def wide(x):
    return x.astype(jnp.float32)


def packed(*flags):
    return sum(jnp.asarray(flag).astype(jnp.int32) << i for i, flag in enumerate(flags)).reshape(1)


def sums_along(blocks, sent, later):
    total, found, span = jnp.sum(blocks, 0), jnp.zeros(sent.shape, jnp.float32), 1
    while span < lax.axis_size("seq"):
        got = wide(passed_along(sent, "seq", -span if later else span))
        found, total = found + got, total + got
        sent = wire(total)
        span *= 2
    return found


def within(blocks, later):
    if blocks.shape[0] == 1:
        return jnp.zeros_like(blocks)
    if later:
        return jnp.cumsum(blocks[::-1], 0)[::-1] - blocks
    return jnp.cumsum(blocks, 0) - blocks


def on_device(queries, keys, values, out_grad):
    rows, width = queries.shape
    pairs, blocks = width // PAIR, rows // BLOCK
    factor = 1.0 / math.sqrt(DH * rows * lax.axis_size("seq"))
    states = jax.ShapeDtypeStruct((blocks, pairs * DH, PAIR), jnp.float32)
    sent = jax.ShapeDtypeStruct((pairs * DH, PAIR), jnp.bfloat16)
    part = jax.ShapeDtypeStruct((rows, width), jnp.float32)
    whole = jax.ShapeDtypeStruct((rows, width), jnp.bfloat16)
    piece = jax.ShapeDtypeStruct((out_grad.shape[0], width), jnp.bfloat16)
    heads, seqs = lax.axis_size("head"), lax.axis_size("seq")
    head = lax.axis_index("head").astype(jnp.int32).reshape(1)

    first = exchange(out_grad, "head", 1)
    pieces = call(
        prepare_kernel,
        [piece] * (heads - 2),
        (head, pltpu.with_memory_space_constraint(out_grad, pltpu.HBM)),
        1.0,
        in_specs=[SMEM, HBM],
        scratch_shapes=[pltpu.SemaphoreType.DMA((heads - 2,))],
    )
    pieces = [exchange(x, "head", d) for d, x in enumerate(pieces, 2)]
    block_state, block_wire = call(state_kernel, [states, sent], (keys, values), 0.3)
    if seqs == 8:
        block_got = exchange(block_wire, "seq", 1)
        block_pair = jnp.sum(block_state, 0) + wide(block_got)
    (attended_part,) = call(
        functools.partial(forward_kernel, factor), [part], (queries, keys, values), 1.0
    )
    grad, grad_state, grad_wire = call(
        gather_kernel,
        [whole, states, sent],
        (head, queries, out_grad, first, *pieces, attended_part),
        0.3,
        in_specs=[SMEM] + [VMEM] * (heads + 1) + [ANY],
    )
    key_part, value_part = call(
        functools.partial(key_value_grad_kernel, factor), [part, part], (queries, keys, values, grad), 1.7
    )
    prefix, suffix = within(block_state, False), within(grad_state, True)
    turn = (lax.axis_index("seq") & 2 != 0).astype(jnp.int32).reshape(1)
    if seqs == 8:
        me = lax.axis_index("seq")
        odd, high, lower = me & 1 != 0, me & 2 != 0, me < 4
        pair_wire = wire(block_pair)
        sends = {1: grad_wire, 2: jnp.where(lower, pair_wire, grad_wire), 3: grad_wire}
        got = {d: exchange(sends[d], "seq", d) for d in (2, 3, 1)}
        other = exchange(jnp.where(lower, grad_wire, pair_wire), "seq", 2)
        got_wide = {d: wide(x) for d, x in got.items()}
        block_total = block_pair + got_wide[2]
        grad_total = jnp.sum(grad_state, 0) + got_wide[1] + got_wide[2] + got_wide[3]
        last_wire = wire(jnp.where(lower, block_total, grad_total))
        (query_part,) = call(
            functools.partial(query_grad_kernel, factor, 1),
            [part],
            (turn, keys, values, grad, got[2]),
            0.3,
            in_specs=[SMEM] + [VMEM] * 3 + [ANY],
        )
        last_wire, query_part, key_part, value_part = lax.optimization_barrier(
            (last_wire, query_part, key_part, value_part)
        )
        last = exchange(last_wire, "seq", 4)
        first_in = (block_got, got[1], got[2], got[3])
        late_in = (block_got, got[1], got[3], other, last)
        early_flags = (lower & odd, ~lower & ~odd, lower == high, ~lower & ~high)
        late_flags = (~lower & odd, lower & ~odd, lower & ~high, lower != high, True)
        plan = ((True, first_in, packed(lower, *early_flags)), (False, late_in, packed(lower, *late_flags)))
        if blocks == 1:
            bases = (jnp.zeros_like(prefix),) * 2
        else:
            bases = jnp.where(lower, prefix, suffix), jnp.where(lower, suffix, prefix)
    else:
        turn, query_part = jnp.zeros_like(turn), jnp.zeros(part.shape, part.dtype)
        bases = (
            prefix + sums_along(block_state, block_wire, False)[None],
            suffix + sums_along(grad_state, grad_wire, True)[None],
        )
        plan = ((True, (), packed(True)), (False, (), packed(True)))
    (query_part,) = call(
        functools.partial(query_grad_kernel, factor, 0),
        [part],
        (turn, keys, values, grad, query_part),
        0.9,
        in_specs=[SMEM] + [VMEM] * 4,
        input_output_aliases={4: 0},
    )
    operands = (queries, keys, values, grad, attended_part, query_part, key_part, value_part)
    results = ()
    for base, (forward, gots, flags) in zip(bases, plan):
        takes = len(gots)
        results = call(
            functools.partial(join_kernel, factor, forward, takes),
            [whole] * 4,
            (flags, base, *gots, *operands, *results),
            0.2,
            in_specs=[SMEM] + [VMEM] * (9 + takes) + [HBM] * len(results),
            out_specs=[HBM] * 4,
            scratch_shapes=[pltpu.VMEM((rows, width), jnp.bfloat16)] * 2
            + [pltpu.SemaphoreType.DMA((blocks, pairs))] * 2,
            input_output_aliases={10 + takes + i: i for i in range(len(results))},
        )
    return tuple(results)


def solution(mesh):
    split = P("seq", "head")
    return jax.shard_map(
        on_device,
        mesh=mesh,
        in_specs=(split, split, split, P(("seq", "head"), None)),
        out_specs=(split, split, split, split),
        check_vma=False,
    )
```

```python
import functools
import math

import jax
import jax.numpy as jnp
from jax import lax
from jax.experimental import pallas as pl
from jax.experimental.pallas import tpu as pltpu
from jax.sharding import PartitionSpec as P

DH = 64
BLOCK = 256
PAIR = 2 * DH
VMEM = pl.BlockSpec(memory_space=pltpu.VMEM)
SMEM = pl.BlockSpec(memory_space=pltpu.SMEM)
HBM = pl.BlockSpec(memory_space=pltpu.HBM)
ANY = pl.BlockSpec(memory_space=pl.ANY)


def dot(a, b, dims):
    return lax.dot_general(a, b, ((dims[:1], dims[1:]), ((), ())), preferred_element_type=jnp.float32)


def first_half(shape):
    return lax.broadcasted_iota(jnp.int32, shape, len(shape) - 1) < DH


def split_pair(x):
    mask = first_half(x.shape)
    zero = jnp.zeros_like(x)
    return jnp.where(mask, x, zero), jnp.where(mask, zero, x)


def pair_state(a, b):
    whole = dot(a, b, (0, 0))
    return jnp.where(first_half((DH, PAIR)), whole[:DH], whole[DH:])


def spread_state(state):
    return jnp.concatenate(split_pair(state), axis=0)


def masked(scores, factor, upper):
    row = lax.broadcasted_iota(jnp.int32, scores.shape, 0)
    col = lax.broadcasted_iota(jnp.int32, scores.shape, 1)
    keep = col >= row if upper else col <= row
    return jnp.where(keep, scores * factor, 0.0).astype(jnp.bfloat16)


def pair_columns(p):
    return slice(p * PAIR, (p + 1) * PAIR)


def state_rows(p):
    return slice(p * DH, (p + 1) * DH)


def block_rows(n):
    return slice(n * BLOCK, (n + 1) * BLOCK)


def state_kernel(a_ref, b_ref, out_ref, wire_ref):
    for p in range(a_ref.shape[1] // PAIR):
        total = 0.0
        for n in range(a_ref.shape[0] // BLOCK):
            state = pair_state(a_ref[block_rows(n), pair_columns(p)], b_ref[block_rows(n), pair_columns(p)])
            out_ref[n, state_rows(p), :] = state
            total = total + state
        wire_ref[state_rows(p), :] = wire(total)


def prepare_kernel(head_ref, g_ref, *refs):
    pieces, sems = refs[:-1], refs[-1]
    width, count = pieces[0].shape[1], len(pieces) + 2
    copies = []
    for d, piece in enumerate(pieces, 2):
        columns = pl.ds(pl.multiple_of(receiver(head_ref[0], d, count) * width, width), width)
        copies.append(pltpu.make_async_copy(g_ref.at[:, columns], piece, sems.at[d - 2]))
    for copy in copies:
        copy.start()
    for copy in copies:
        copy.wait()


def gather_kernel(head_ref, q_ref, g_ref, first_ref, *refs):
    pieces, (_, grad_ref, out_ref, wire_ref) = refs[:-4], refs[-4:]
    rows, width, count = g_ref.shape[0], q_ref.shape[1], len(pieces) + 2
    columns = pl.ds(pl.multiple_of(head_ref[0] * width, width), width)
    pieces = (g_ref.at[:, columns], first_ref.at[:, columns], *pieces)
    for d, piece in enumerate(pieces):
        source = sender(head_ref[0], d, count)
        grad_ref[pl.ds(pl.multiple_of(source * rows, rows), rows), :] = piece[...]
    state_kernel(q_ref, grad_ref, out_ref, wire_ref)


def forward_kernel(factor, q_ref, k_ref, v_ref, att_ref):
    for n in range(q_ref.shape[0] // BLOCK):
        for p in range(q_ref.shape[1] // PAIR):
            at = (block_rows(n), pair_columns(p))
            q, k, v = q_ref[at], k_ref[at], v_ref[at]
            total = 0.0
            for q_head, v_head in zip(split_pair(q), split_pair(v)):
                probs = masked(dot(q_head, k, (1, 1)), factor, False)
                total = total + dot(probs, v_head, (1, 0))
            att_ref[at] = total


def query_grad_kernel(factor, k_ref, v_ref, g_ref, dq_ref):
    for n in range(k_ref.shape[0] // BLOCK):
        for p in range(k_ref.shape[1] // PAIR):
            at = (block_rows(n), pair_columns(p))
            k, v, g = k_ref[at], v_ref[at], g_ref[at]
            total = 0.0
            for k_head, g_head in zip(split_pair(k), split_pair(g)):
                dprobs = masked(dot(g_head, v, (1, 1)), factor, False)
                total = total + dot(dprobs, k_head, (1, 0))
            dq_ref[at] = total


def key_value_grad_kernel(factor, q_ref, k_ref, v_ref, g_ref, dk_ref, dv_ref):
    for n in range(q_ref.shape[0] // BLOCK):
        for p in range(q_ref.shape[1] // PAIR):
            at = (block_rows(n), pair_columns(p))
            q, k, v, g = q_ref[at], k_ref[at], v_ref[at], g_ref[at]
            dk = dv = 0.0
            for q_head, k_head, v_head, g_head in zip(*map(split_pair, (q, k, v, g))):
                probs_t = masked(dot(k_head, q, (1, 1)), factor, True)
                dv = dv + dot(probs_t, g_head, (1, 0))
                dprobs_t = masked(dot(v_head, g, (1, 1)), factor, True)
                dk = dk + dot(dprobs_t, q_head, (1, 0))
            dk_ref[at] = dk
            dv_ref[at] = dv


def join(factor, state_of, a, b):
    copies = []
    for n in range(a[0].shape[0] // BLOCK):
        for p in range(a[0].shape[1] // PAIR):
            at = (block_rows(n), pair_columns(p))
            state = spread_state(state_of(n, state_rows(p)))
            for (x_ref, part_ref, held, out_ref, sems), side in ((a, 0), (b, 1)):
                added = factor * dot(x_ref[at], state, (1, side))
                held[at] = (part_ref[at] + added).astype(jnp.bfloat16)
                copy = pltpu.make_async_copy(held.at[at], out_ref.at[at], sems.at[n, p])
                copy.start()
                copies.append(copy)
    for copy in copies:
        copy.wait()


def join_kernel(factor, forward, flags_ref, state_of, parts, refs):
    q_ref, k_ref, v_ref, g_ref, att_part, dq_part, dk_part, dv_part = parts
    att_ref, dq_ref, dk_ref, dv_ref, a_held, b_held, a_sems, b_sems = refs
    is_forward = flags_ref[0] & 1 == int(forward)

    @pl.when(is_forward)
    def _():
        a = (q_ref, att_part, a_held, att_ref, a_sems)
        b = (g_ref, dq_part, b_held, dq_ref, b_sems)
        join(factor, state_of, a, b)

    @pl.when(jnp.logical_not(is_forward))
    def _():
        a = (k_ref, dv_part, a_held, dv_ref, a_sems)
        b = (v_ref, dk_part, b_held, dk_ref, b_sems)
        join(factor, state_of, a, b)


def early_kernel(factor, flags_ref, early_ref, late_ref, *refs):
    gots, parts, late_out_ref, rest = refs[:-17], refs[-17:-9], refs[-5], (*refs[-9:-5], *refs[-4:])

    def marked(base_ref, n, rows, first):
        state = base_ref[n, rows, :]
        for i, got_ref in enumerate(gots, first):
            state = state + jnp.where(flags_ref[0] >> i & 1 == 1, wide(got_ref[rows, :]), 0.0)
        return state

    for n in range(late_ref.shape[0]):
        for p in range(late_ref.shape[1] // DH):
            late_out_ref[n, state_rows(p), :] = marked(late_ref, n, state_rows(p), 1 + len(gots))
    join_kernel(factor, True, flags_ref, lambda n, rows: wire(marked(early_ref, n, rows, 1)), parts, rest)


def late_kernel(factor, flags_ref, late_ref, *refs):
    lasts, parts, rest = refs[:-20], refs[-20:-12], refs[-8:]

    def state_of(n, rows):
        return wire(sum((wide(last_ref[rows, :]) for last_ref in lasts), late_ref[n, rows, :]))

    join_kernel(factor, False, flags_ref, state_of, parts, rest)


def in_pairs(count):
    return count & (count - 1) == 0


def receiver(index, d, count):
    return index ^ d if in_pairs(count) else lax.rem(index + d, count)


def sender(index, d, count):
    return index ^ d if in_pairs(count) else lax.rem(index - d + count, count)


def exchange(x, axis, d):
    count = lax.axis_size(axis)
    return lax.ppermute(x, axis, [(i, i ^ d if in_pairs(count) else (i + d) % count) for i in range(count)])


def passed_along(x, axis, step):
    count = lax.axis_size(axis)
    return lax.ppermute(x, axis, [(i, i + step) for i in range(count) if 0 <= i + step < count])


def call(kernel, out_shapes, operands, microseconds, out_specs=None, in_specs=None, **options):
    return pl.pallas_call(
        kernel,
        out_shape=out_shapes,
        in_specs=in_specs or [VMEM] * len(operands),
        out_specs=out_specs or [VMEM] * len(out_shapes),
        compiler_params=pltpu.CompilerParams(vmem_limit_bytes=24 * 1024 * 1024),
        cost_estimate=pl.CostEstimate(flops=int(1.15e9 * microseconds), bytes_accessed=0, transcendentals=0),
        **options,
    )(*operands)


def wire(x):
    return x.astype(jnp.bfloat16)


def wide(x):
    return x.astype(jnp.float32)


def packed(*flags):
    return sum(jnp.asarray(flag).astype(jnp.int32) << i for i, flag in enumerate(flags)).reshape(1)


def sums_along(blocks, sent, later):
    total, found, span = jnp.sum(blocks, 0), jnp.zeros(sent.shape, jnp.float32), 1
    while span < lax.axis_size("seq"):
        got = wide(passed_along(sent, "seq", -span if later else span))
        found, total = found + got, total + got
        sent = wire(total)
        span *= 2
    return found


def within(blocks, later):
    if blocks.shape[0] == 1:
        return jnp.zeros_like(blocks)
    if later:
        return jnp.cumsum(blocks[::-1], 0)[::-1] - blocks
    return jnp.cumsum(blocks, 0) - blocks


def on_device(queries, keys, values, out_grad):
    rows, width = queries.shape
    pairs, blocks = width // PAIR, rows // BLOCK
    factor = 1.0 / math.sqrt(DH * rows * lax.axis_size("seq"))
    states = jax.ShapeDtypeStruct((blocks, pairs * DH, PAIR), jnp.float32)
    sent = jax.ShapeDtypeStruct((pairs * DH, PAIR), jnp.bfloat16)
    part = jax.ShapeDtypeStruct((rows, width), jnp.float32)
    whole = jax.ShapeDtypeStruct((rows, width), jnp.bfloat16)
    piece = jax.ShapeDtypeStruct((out_grad.shape[0], width), jnp.bfloat16)
    heads, seqs = lax.axis_size("head"), lax.axis_size("seq")
    head = lax.axis_index("head").astype(jnp.int32).reshape(1)

    first = exchange(out_grad, "head", 1)
    pieces = call(
        prepare_kernel,
        [piece] * (heads - 2),
        (head, pltpu.with_memory_space_constraint(out_grad, pltpu.HBM)),
        1.0,
        in_specs=[SMEM, HBM],
        scratch_shapes=[pltpu.SemaphoreType.DMA((heads - 2,))],
    )
    pieces = [exchange(x, "head", d) for d, x in enumerate(pieces, 2)]
    block_state, block_wire = call(state_kernel, [states, sent], (keys, values), 0.3)
    if seqs == 8:
        block_got = exchange(block_wire, "seq", 1)
        block_pair = jnp.sum(block_state, 0) + wide(block_got)
    (attended_part,) = call(
        functools.partial(forward_kernel, factor), [part], (queries, keys, values), 1.0
    )
    grad, grad_state, grad_wire = call(
        gather_kernel,
        [whole, states, sent],
        (head, queries, out_grad, first, *pieces, attended_part),
        0.3,
        in_specs=[SMEM] + [VMEM] * (heads + 1) + [ANY],
    )
    key_part, value_part = call(
        functools.partial(key_value_grad_kernel, factor), [part, part], (queries, keys, values, grad), 1.7
    )
    prefix, suffix = within(block_state, False), within(grad_state, True)
    if seqs == 8:
        me = lax.axis_index("seq")
        odd, high, lower = me & 1 != 0, me & 2 != 0, me < 4
        pair_wire = wire(block_pair)
        sends = {2: jnp.where(lower, pair_wire, grad_wire), 3: grad_wire}
        sends[1], sends[2] = lax.optimization_barrier((grad_wire, sends[2]))
        got = {d: exchange(sends[d], "seq", d) for d in (2, 3, 1)}
        other = exchange(jnp.where(lower, grad_wire, pair_wire), "seq", 2)
        got_wide = {d: wide(x) for d, x in got.items()}
        block_total = block_pair + got_wide[2]
        grad_total = jnp.sum(grad_state, 0) + got_wide[2] + got_wide[1] + got_wide[3]
        last_wire = wire(jnp.where(lower, block_total, grad_total))
        last_wire, key_part, value_part = lax.optimization_barrier((last_wire, key_part, value_part))
        last = exchange(last_wire, "seq", 4)
        gots, lasts = (block_got, got[2], got[1], got[3], other), (last,)
        flags = (
            lower,
            *(lower & odd, lower == high, ~lower & ~odd, ~lower & ~high, False),
            *(~lower & odd, False, lower & ~odd, lower & ~high, lower != high),
        )
        early, late = jnp.where(lower, prefix, suffix), jnp.where(lower, suffix, prefix)
    else:
        gots, lasts, flags = (), (), (True,)
        early = prefix + sums_along(block_state, block_wire, False)[None]
        late = suffix + sums_along(grad_state, grad_wire, True)[None]
    (query_part,) = call(functools.partial(query_grad_kernel, factor), [part], (keys, values, grad), 0.9)
    operands = (queries, keys, values, grad, attended_part, query_part, key_part, value_part)
    held = [pltpu.VMEM((rows, width), jnp.bfloat16)] * 2 + [pltpu.SemaphoreType.DMA((blocks, pairs))] * 2
    *results, late = call(
        functools.partial(early_kernel, factor),
        [whole] * 4 + [states],
        (packed(*flags), early, late, *gots, *operands),
        0.2,
        in_specs=[SMEM] + [VMEM] * (10 + len(gots)),
        out_specs=[HBM] * 4 + [VMEM],
        scratch_shapes=held,
    )
    results = call(
        functools.partial(late_kernel, factor),
        [whole] * 4,
        (packed(*flags), late, *lasts, *operands, *results),
        0.2,
        in_specs=[SMEM] + [VMEM] * (9 + len(lasts)) + [HBM] * 4,
        out_specs=[HBM] * 4,
        scratch_shapes=held,
        input_output_aliases={10 + len(lasts) + i: i for i in range(4)},
    )
    return tuple(results)


def solution(mesh):
    split = P("seq", "head")
    return jax.shard_map(
        on_device,
        mesh=mesh,
        in_specs=(split, split, split, P(("seq", "head"), None)),
        out_specs=(split, split, split, split),
        check_vma=False,
    )
```

```python
import functools
import math

import jax
import jax.numpy as jnp
from jax import lax
from jax.experimental import pallas as pl
from jax.experimental.pallas import tpu as pltpu
from jax.sharding import PartitionSpec as P

DH = 64
BLOCK = 256
PAIR = 2 * DH
VMEM = pl.BlockSpec(memory_space=pltpu.VMEM)
SMEM = pl.BlockSpec(memory_space=pltpu.SMEM)
HBM = pl.BlockSpec(memory_space=pltpu.HBM)
ANY = pl.BlockSpec(memory_space=pl.ANY)


def dot(a, b, dims):
    return lax.dot_general(a, b, ((dims[:1], dims[1:]), ((), ())), preferred_element_type=jnp.float32)


def first_half(shape):
    return lax.broadcasted_iota(jnp.int32, shape, len(shape) - 1) < DH


def split_pair(x):
    mask = first_half(x.shape)
    zero = jnp.zeros_like(x)
    return jnp.where(mask, x, zero), jnp.where(mask, zero, x)


def pair_state(a, b):
    whole = dot(a, b, (0, 0))
    return jnp.where(first_half((DH, PAIR)), whole[:DH], whole[DH:])


def spread_state(state):
    return jnp.concatenate(split_pair(state), axis=0)


def masked(scores, factor, upper):
    row = lax.broadcasted_iota(jnp.int32, scores.shape, 0)
    col = lax.broadcasted_iota(jnp.int32, scores.shape, 1)
    keep = col >= row if upper else col <= row
    return jnp.where(keep, scores * factor, 0.0).astype(jnp.bfloat16)


def pair_columns(p):
    return slice(p * PAIR, (p + 1) * PAIR)


def state_rows(p):
    return slice(p * DH, (p + 1) * DH)


def block_rows(n):
    return slice(n * BLOCK, (n + 1) * BLOCK)


def state_kernel(a_ref, b_ref, out_ref, wire_ref):
    for p in range(a_ref.shape[1] // PAIR):
        total = 0.0
        for n in range(a_ref.shape[0] // BLOCK):
            state = pair_state(a_ref[block_rows(n), pair_columns(p)], b_ref[block_rows(n), pair_columns(p)])
            out_ref[n, state_rows(p), :] = state
            total = total + state
        wire_ref[state_rows(p), :] = wire(total)


def first_state_kernel(k_ref, v_ref, _, out_ref, wire_ref):
    state_kernel(k_ref, v_ref, out_ref, wire_ref)


def prepare_kernel(head_ref, g_ref, *refs):
    pieces, sems = refs[:-1], refs[-1]
    width, count = pieces[0].shape[1], len(pieces)
    copies = []
    for d, piece in enumerate(pieces, 1):
        target = receiver(head_ref[0], d, count) if d < count else head_ref[0]
        columns = pl.ds(pl.multiple_of(target * width, width), width)
        copies.append(pltpu.make_async_copy(g_ref.at[:, columns], piece, sems.at[d - 1]))
    for copy in copies:
        copy.start()
    for copy in copies:
        copy.wait()


def gather_kernel(head_ref, q_ref, *refs):
    pieces, (_, grad_ref, out_ref, wire_ref) = refs[:-4], refs[-4:]
    rows, count = pieces[0].shape[0], len(pieces)
    for d, piece in zip((*range(2, count), 1, 0), pieces):
        source = sender(head_ref[0], d, count)
        grad_ref[pl.ds(pl.multiple_of(source * rows, rows), rows), :] = piece[...]
    state_kernel(q_ref, grad_ref, out_ref, wire_ref)


def forward_kernel(factor, q_ref, k_ref, v_ref, att_ref):
    for n in range(q_ref.shape[0] // BLOCK):
        for p in range(q_ref.shape[1] // PAIR):
            at = (block_rows(n), pair_columns(p))
            q, k, v = q_ref[at], k_ref[at], v_ref[at]
            total = 0.0
            for q_head, v_head in zip(split_pair(q), split_pair(v)):
                probs = masked(dot(q_head, k, (1, 1)), factor, False)
                total = total + dot(probs, v_head, (1, 0))
            att_ref[at] = total


def query_grad_kernel(factor, k_ref, v_ref, g_ref, dq_ref):
    for n in range(k_ref.shape[0] // BLOCK):
        for p in range(k_ref.shape[1] // PAIR):
            at = (block_rows(n), pair_columns(p))
            k, v, g = k_ref[at], v_ref[at], g_ref[at]
            total = 0.0
            for k_head, g_head in zip(split_pair(k), split_pair(g)):
                dprobs = masked(dot(g_head, v, (1, 1)), factor, False)
                total = total + dot(dprobs, k_head, (1, 0))
            dq_ref[at] = total


def key_value_grad_kernel(factor, q_ref, k_ref, v_ref, g_ref, dk_ref, dv_ref):
    for n in range(q_ref.shape[0] // BLOCK):
        for p in range(q_ref.shape[1] // PAIR):
            at = (block_rows(n), pair_columns(p))
            q, k, v, g = q_ref[at], k_ref[at], v_ref[at], g_ref[at]
            dk = dv = 0.0
            for q_head, k_head, v_head, g_head in zip(*map(split_pair, (q, k, v, g))):
                probs_t = masked(dot(k_head, q, (1, 1)), factor, True)
                dv = dv + dot(probs_t, g_head, (1, 0))
                dprobs_t = masked(dot(v_head, g, (1, 1)), factor, True)
                dk = dk + dot(dprobs_t, q_head, (1, 0))
            dk_ref[at] = dk
            dv_ref[at] = dv


def join(factor, state_of, a, b):
    copies = []
    for n in range(a[0].shape[0] // BLOCK):
        for p in range(a[0].shape[1] // PAIR):
            at = (block_rows(n), pair_columns(p))
            state = spread_state(state_of(n, state_rows(p)))
            for (x_ref, part_ref, held, out_ref, sems), side in ((a, 0), (b, 1)):
                added = factor * dot(x_ref[at], state, (1, side))
                held[at] = (part_ref[at] + added).astype(jnp.bfloat16)
                copy = pltpu.make_async_copy(held.at[at], out_ref.at[at], sems.at[n, p])
                copy.start()
                copies.append(copy)
    for copy in copies:
        copy.wait()


def join_kernel(factor, forward, flags_ref, state_of, parts, refs):
    q_ref, k_ref, v_ref, g_ref, att_part, dq_part, dk_part, dv_part = parts
    att_ref, dq_ref, dk_ref, dv_ref, a_held, b_held, a_sems, b_sems = refs
    is_forward = flags_ref[0] & 1 == int(forward)

    @pl.when(is_forward)
    def _():
        a = (q_ref, att_part, a_held, att_ref, a_sems)
        b = (g_ref, dq_part, b_held, dq_ref, b_sems)
        join(factor, state_of, a, b)

    @pl.when(jnp.logical_not(is_forward))
    def _():
        a = (k_ref, dv_part, a_held, dv_ref, a_sems)
        b = (v_ref, dk_part, b_held, dk_ref, b_sems)
        join(factor, state_of, a, b)


def early_kernel(factor, flags_ref, early_ref, late_ref, *refs):
    gots, parts, late_out_ref, rest = refs[:-17], refs[-17:-9], refs[-5], (*refs[-9:-5], *refs[-4:])

    def marked(base_ref, n, rows, first):
        state = base_ref[n, rows, :]
        for i, got_ref in enumerate(gots, first):
            state = state + jnp.where(flags_ref[0] >> i & 1 == 1, wide(got_ref[rows, :]), 0.0)
        return state

    for n in range(late_ref.shape[0]):
        for p in range(late_ref.shape[1] // DH):
            late_out_ref[n, state_rows(p), :] = marked(late_ref, n, state_rows(p), 1 + len(gots))
    join_kernel(factor, True, flags_ref, lambda n, rows: wire(marked(early_ref, n, rows, 1)), parts, rest)


def late_kernel(factor, flags_ref, late_ref, *refs):
    lasts, parts, rest = refs[:-20], refs[-20:-12], refs[-8:]

    def state_of(n, rows):
        return wire(sum((wide(last_ref[rows, :]) for last_ref in lasts), late_ref[n, rows, :]))

    join_kernel(factor, False, flags_ref, state_of, parts, rest)


def in_pairs(count):
    return count & (count - 1) == 0


def receiver(index, d, count):
    return index ^ d if in_pairs(count) else lax.rem(index + d, count)


def sender(index, d, count):
    return index ^ d if in_pairs(count) else lax.rem(index - d + count, count)


def exchange(x, axis, d):
    count = lax.axis_size(axis)
    return lax.ppermute(x, axis, [(i, i ^ d if in_pairs(count) else (i + d) % count) for i in range(count)])


def passed_along(x, axis, step):
    count = lax.axis_size(axis)
    return lax.ppermute(x, axis, [(i, i + step) for i in range(count) if 0 <= i + step < count])


def call(kernel, out_shapes, operands, microseconds, out_specs=None, in_specs=None, **options):
    return pl.pallas_call(
        kernel,
        out_shape=out_shapes,
        in_specs=in_specs or [VMEM] * len(operands),
        out_specs=out_specs or [VMEM] * len(out_shapes),
        compiler_params=pltpu.CompilerParams(vmem_limit_bytes=24 * 1024 * 1024),
        cost_estimate=pl.CostEstimate(flops=int(1.15e9 * microseconds), bytes_accessed=0, transcendentals=0),
        **options,
    )(*operands)


def wire(x):
    return x.astype(jnp.bfloat16)


def wide(x):
    return x.astype(jnp.float32)


def packed(*flags):
    return sum(jnp.asarray(flag).astype(jnp.int32) << i for i, flag in enumerate(flags)).reshape(1)


def sums_along(blocks, sent, later):
    total, found, span = jnp.sum(blocks, 0), jnp.zeros(sent.shape, jnp.float32), 1
    while span < lax.axis_size("seq"):
        got = wide(passed_along(sent, "seq", -span if later else span))
        found, total = found + got, total + got
        sent = wire(total)
        span *= 2
    return found


def within(blocks, later):
    if blocks.shape[0] == 1:
        return jnp.zeros_like(blocks)
    if later:
        return jnp.cumsum(blocks[::-1], 0)[::-1] - blocks
    return jnp.cumsum(blocks, 0) - blocks


def on_device(queries, keys, values, out_grad):
    rows, width = queries.shape
    pairs, blocks = width // PAIR, rows // BLOCK
    factor = 1.0 / math.sqrt(DH * rows * lax.axis_size("seq"))
    states = jax.ShapeDtypeStruct((blocks, pairs * DH, PAIR), jnp.float32)
    sent = jax.ShapeDtypeStruct((pairs * DH, PAIR), jnp.bfloat16)
    part = jax.ShapeDtypeStruct((rows, width), jnp.float32)
    whole = jax.ShapeDtypeStruct((rows, width), jnp.bfloat16)
    piece = jax.ShapeDtypeStruct((out_grad.shape[0], width), jnp.bfloat16)
    heads, seqs = lax.axis_size("head"), lax.axis_size("seq")
    head = lax.axis_index("head").astype(jnp.int32).reshape(1)

    *pieces, own = call(
        prepare_kernel,
        [piece] * heads,
        (head, pltpu.with_memory_space_constraint(out_grad, pltpu.HBM)),
        1.0,
        in_specs=[SMEM, HBM],
        scratch_shapes=[pltpu.SemaphoreType.DMA((heads,))],
    )
    pieces = [exchange(x, "head", d) for d, x in enumerate(pieces, 1)]
    block_state, block_wire = call(
        first_state_kernel, [states, sent], (keys, values, own), 0.3, in_specs=[VMEM, VMEM, ANY]
    )
    if seqs == 8:
        block_got = exchange(block_wire, "seq", 1)
        block_pair = jnp.sum(block_state, 0) + wide(block_got)
    (attended_part,) = call(
        functools.partial(forward_kernel, factor), [part], (queries, keys, values), 1.0
    )
    grad, grad_state, grad_wire = call(
        gather_kernel,
        [whole, states, sent],
        (head, queries, *pieces[1:], pieces[0], own, attended_part),
        0.3,
        in_specs=[SMEM] + [VMEM] * (heads + 1) + [ANY],
    )
    key_part, value_part = call(
        functools.partial(key_value_grad_kernel, factor), [part, part], (queries, keys, values, grad), 1.7
    )
    prefix, suffix = within(block_state, False), within(grad_state, True)
    if seqs == 8:
        me = lax.axis_index("seq")
        odd, high, lower = me & 1 != 0, me & 2 != 0, me < 4
        pair_wire = wire(block_pair)
        sends = {2: jnp.where(lower, pair_wire, grad_wire), 3: grad_wire}
        sends[1], sends[2] = lax.optimization_barrier((grad_wire, sends[2]))
        got = {d: exchange(sends[d], "seq", d) for d in (2, 3, 1)}
        other = exchange(jnp.where(lower, grad_wire, pair_wire), "seq", 2)
        got_wide = {d: wide(x) for d, x in got.items()}
        block_total = block_pair + got_wide[2]
        grad_total = jnp.sum(grad_state, 0) + got_wide[2] + got_wide[1] + got_wide[3]
        last_wire = wire(jnp.where(lower, block_total, grad_total))
        last_wire, key_part, value_part = lax.optimization_barrier((last_wire, key_part, value_part))
        last = exchange(last_wire, "seq", 4)
        gots, lasts = (block_got, got[2], got[1], got[3], other), (last,)
        flags = (
            lower,
            *(lower & odd, lower == high, ~lower & ~odd, ~lower & ~high, False),
            *(~lower & odd, False, lower & ~odd, lower & ~high, lower != high),
        )
        early, late = jnp.where(lower, prefix, suffix), jnp.where(lower, suffix, prefix)
    else:
        gots, lasts, flags = (), (), (True,)
        early = prefix + sums_along(block_state, block_wire, False)[None]
        late = suffix + sums_along(grad_state, grad_wire, True)[None]
    (query_part,) = call(functools.partial(query_grad_kernel, factor), [part], (keys, values, grad), 0.9)
    operands = (queries, keys, values, grad, attended_part, query_part, key_part, value_part)
    held = [pltpu.VMEM((rows, width), jnp.bfloat16)] * 2 + [pltpu.SemaphoreType.DMA((blocks, pairs))] * 2
    *results, late = call(
        functools.partial(early_kernel, factor),
        [whole] * 4 + [states],
        (packed(*flags), early, late, *gots, *operands),
        0.2,
        in_specs=[SMEM] + [VMEM] * (10 + len(gots)),
        out_specs=[HBM] * 4 + [VMEM],
        scratch_shapes=held,
    )
    results = call(
        functools.partial(late_kernel, factor),
        [whole] * 4,
        (packed(*flags), late, *lasts, *operands, *results),
        0.2,
        in_specs=[SMEM] + [VMEM] * (9 + len(lasts)) + [HBM] * 4,
        out_specs=[HBM] * 4,
        scratch_shapes=held,
        input_output_aliases={10 + len(lasts) + i: i for i in range(4)},
    )
    return tuple(results)


def solution(mesh):
    split = P("seq", "head")
    return jax.shard_map(
        on_device,
        mesh=mesh,
        in_specs=(split, split, split, P(("seq", "head"), None)),
        out_specs=(split, split, split, split),
        check_vma=False,
    )
```

```python
import functools
import math

import jax
import jax.numpy as jnp
from jax import lax
from jax.experimental import pallas as pl
from jax.experimental.pallas import tpu as pltpu
from jax.sharding import PartitionSpec as P

DH = 64
BLOCK = 256
PAIR = 2 * DH
VMEM = pl.BlockSpec(memory_space=pltpu.VMEM)
SMEM = pl.BlockSpec(memory_space=pltpu.SMEM)
HBM = pl.BlockSpec(memory_space=pltpu.HBM)
ANY = pl.BlockSpec(memory_space=pl.ANY)


def dot(a, b, dims):
    return lax.dot_general(a, b, ((dims[:1], dims[1:]), ((), ())), preferred_element_type=jnp.float32)


def first_half(shape):
    return lax.broadcasted_iota(jnp.int32, shape, len(shape) - 1) < DH


def split_pair(x):
    mask = first_half(x.shape)
    zero = jnp.zeros_like(x)
    return jnp.where(mask, x, zero), jnp.where(mask, zero, x)


def pair_state(a, b):
    whole = dot(a, b, (0, 0))
    return jnp.where(first_half((DH, PAIR)), whole[:DH], whole[DH:])


def spread_state(state):
    return jnp.concatenate(split_pair(state), axis=0)


def masked(scores, factor, upper):
    row = lax.broadcasted_iota(jnp.int32, scores.shape, 0)
    col = lax.broadcasted_iota(jnp.int32, scores.shape, 1)
    keep = col >= row if upper else col <= row
    return jnp.where(keep, scores * factor, 0.0).astype(jnp.bfloat16)


def pair_columns(p):
    return slice(p * PAIR, (p + 1) * PAIR)


def state_rows(p):
    return slice(p * DH, (p + 1) * DH)


def block_rows(n):
    return slice(n * BLOCK, (n + 1) * BLOCK)


def state_kernel(a_ref, b_ref, out_ref, wire_ref):
    for p in range(a_ref.shape[1] // PAIR):
        total = 0.0
        for n in range(a_ref.shape[0] // BLOCK):
            state = pair_state(a_ref[block_rows(n), pair_columns(p)], b_ref[block_rows(n), pair_columns(p)])
            out_ref[n, state_rows(p), :] = state
            total = total + state
        wire_ref[state_rows(p), :] = wire(total)


def first_state_kernel(k_ref, v_ref, _, out_ref, wire_ref):
    state_kernel(k_ref, v_ref, out_ref, wire_ref)


def cut(head_ref, g_ref, pieces, steps, count, sems):
    width, copies = pieces[0].shape[1], []
    for i, (d, piece) in enumerate(zip(steps, pieces)):
        target = receiver(head_ref[0], d, count) if d else head_ref[0]
        columns = pl.ds(pl.multiple_of(target * width, width), width)
        copies.append(pltpu.make_async_copy(g_ref.at[:, columns], piece, sems.at[i]))
    for copy in copies:
        copy.start()
    for copy in copies:
        copy.wait()


def prepare_kernel(steps, count, head_ref, g_ref, *refs):
    cut(head_ref, g_ref, refs[-1 - len(steps) : -1], steps, count, refs[-1])


def transpose_kernel(x_ref, out_ref):
    for p in range(x_ref.shape[1] // PAIR):
        out_ref[pair_columns(p), :] = x_ref[:, pair_columns(p)].T


def gather_kernel(head_ref, qt_ref, *refs):
    pieces, (_, grad_ref, out_ref, wire_ref) = refs[:-4], refs[-4:]
    rows, count = pieces[0].shape[0], len(pieces)
    for d, piece in zip((*range(2, count), 1, 0), pieces):
        source = sender(head_ref[0], d, count)
        grad_ref[pl.ds(pl.multiple_of(source * rows, rows), rows), :] = piece[...]
    for p in range(qt_ref.shape[0] // PAIR):
        total = 0.0
        for n in range(grad_ref.shape[0] // BLOCK):
            whole = dot(qt_ref[pair_columns(p), block_rows(n)], grad_ref[block_rows(n), pair_columns(p)], (1, 0))
            state = jnp.where(first_half((DH, PAIR)), whole[:DH], whole[DH:])
            out_ref[n, state_rows(p), :] = state
            total = total + state
        wire_ref[state_rows(p), :] = wire(total)


def forward_kernel(factor, q_ref, k_ref, v_ref, att_ref):
    for n in range(q_ref.shape[0] // BLOCK):
        for p in range(q_ref.shape[1] // PAIR):
            at = (block_rows(n), pair_columns(p))
            q, k, v = q_ref[at], k_ref[at], v_ref[at]
            total = 0.0
            for q_head, v_head in zip(split_pair(q), split_pair(v)):
                probs = masked(dot(q_head, k, (1, 1)), factor, False)
                total = total + dot(probs, v_head, (1, 0))
            att_ref[at] = total


def query_grad_kernel(factor, k_ref, v_ref, g_ref, dq_ref):
    for n in range(k_ref.shape[0] // BLOCK):
        for p in range(k_ref.shape[1] // PAIR):
            at = (block_rows(n), pair_columns(p))
            k, v, g = k_ref[at], v_ref[at], g_ref[at]
            total = 0.0
            for k_head, g_head in zip(split_pair(k), split_pair(g)):
                dprobs = masked(dot(g_head, v, (1, 1)), factor, False)
                total = total + dot(dprobs, k_head, (1, 0))
            dq_ref[at] = total


def key_value_grad_kernel(factor, q_ref, k_ref, v_ref, g_ref, dk_ref, dv_ref):
    for n in range(q_ref.shape[0] // BLOCK):
        for p in range(q_ref.shape[1] // PAIR):
            at = (block_rows(n), pair_columns(p))
            q, k, v, g = q_ref[at], k_ref[at], v_ref[at], g_ref[at]
            dk = dv = 0.0
            for q_head, k_head, v_head, g_head in zip(*map(split_pair, (q, k, v, g))):
                probs_t = masked(dot(k_head, q, (1, 1)), factor, True)
                dv = dv + dot(probs_t, g_head, (1, 0))
                dprobs_t = masked(dot(v_head, g, (1, 1)), factor, True)
                dk = dk + dot(dprobs_t, q_head, (1, 0))
            dk_ref[at] = dk
            dv_ref[at] = dv


def join(factor, state_of, a, b):
    copies = []
    for n in range(a[0].shape[0] // BLOCK):
        for p in range(a[0].shape[1] // PAIR):
            at = (block_rows(n), pair_columns(p))
            state = spread_state(state_of(n, state_rows(p)))
            for (x_ref, part_ref, held, out_ref, sems), side in ((a, 0), (b, 1)):
                added = factor * dot(x_ref[at], state, (1, side))
                held[at] = (part_ref[at] + added).astype(jnp.bfloat16)
                copy = pltpu.make_async_copy(held.at[at], out_ref.at[at], sems.at[n, p])
                copy.start()
                copies.append(copy)
    for copy in copies:
        copy.wait()


def join_kernel(factor, forward, flags_ref, state_of, parts, refs):
    q_ref, k_ref, v_ref, g_ref, att_part, dq_part, dk_part, dv_part = parts
    att_ref, dq_ref, dk_ref, dv_ref, a_held, b_held, a_sems, b_sems = refs
    is_forward = flags_ref[0] & 1 == int(forward)

    @pl.when(is_forward)
    def _():
        a = (q_ref, att_part, a_held, att_ref, a_sems)
        b = (g_ref, dq_part, b_held, dq_ref, b_sems)
        join(factor, state_of, a, b)

    @pl.when(jnp.logical_not(is_forward))
    def _():
        a = (k_ref, dv_part, a_held, dv_ref, a_sems)
        b = (v_ref, dk_part, b_held, dk_ref, b_sems)
        join(factor, state_of, a, b)


def early_kernel(factor, flags_ref, early_ref, late_ref, *refs):
    gots, parts, late_out_ref, rest = refs[:-17], refs[-17:-9], refs[-5], (*refs[-9:-5], *refs[-4:])

    def marked(base_ref, n, rows, first):
        state = base_ref[n, rows, :]
        for i, got_ref in enumerate(gots, first):
            state = state + jnp.where(flags_ref[0] >> i & 1 == 1, wide(got_ref[rows, :]), 0.0)
        return state

    for n in range(late_ref.shape[0]):
        for p in range(late_ref.shape[1] // DH):
            late_out_ref[n, state_rows(p), :] = marked(late_ref, n, state_rows(p), 1 + len(gots))
    join_kernel(factor, True, flags_ref, lambda n, rows: wire(marked(early_ref, n, rows, 1)), parts, rest)


def late_kernel(factor, flags_ref, late_ref, *refs):
    lasts, parts, rest = refs[:-20], refs[-20:-12], refs[-8:]

    def state_of(n, rows):
        return wire(sum((wide(last_ref[rows, :]) for last_ref in lasts), late_ref[n, rows, :]))

    join_kernel(factor, False, flags_ref, state_of, parts, rest)


def in_pairs(count):
    return count & (count - 1) == 0


def receiver(index, d, count):
    return index ^ d if in_pairs(count) else lax.rem(index + d, count)


def sender(index, d, count):
    return index ^ d if in_pairs(count) else lax.rem(index - d + count, count)


def exchange(x, axis, d):
    count = lax.axis_size(axis)
    return lax.ppermute(x, axis, [(i, i ^ d if in_pairs(count) else (i + d) % count) for i in range(count)])


def passed_along(x, axis, step):
    count = lax.axis_size(axis)
    return lax.ppermute(x, axis, [(i, i + step) for i in range(count) if 0 <= i + step < count])


def call(kernel, out_shapes, operands, microseconds, out_specs=None, in_specs=None, **options):
    return pl.pallas_call(
        kernel,
        out_shape=out_shapes,
        in_specs=in_specs or [VMEM] * len(operands),
        out_specs=out_specs or [VMEM] * len(out_shapes),
        compiler_params=pltpu.CompilerParams(vmem_limit_bytes=24 * 1024 * 1024),
        cost_estimate=pl.CostEstimate(flops=int(1.15e9 * microseconds), bytes_accessed=0, transcendentals=0),
        **options,
    )(*operands)


def wire(x):
    return x.astype(jnp.bfloat16)


def wide(x):
    return x.astype(jnp.float32)


def packed(*flags):
    return sum(jnp.asarray(flag).astype(jnp.int32) << i for i, flag in enumerate(flags)).reshape(1)


def sums_along(blocks, sent, later):
    total, found, span = jnp.sum(blocks, 0), jnp.zeros(sent.shape, jnp.float32), 1
    while span < lax.axis_size("seq"):
        got = wide(passed_along(sent, "seq", -span if later else span))
        found, total = found + got, total + got
        sent = wire(total)
        span *= 2
    return found


def within(blocks, later):
    if blocks.shape[0] == 1:
        return jnp.zeros_like(blocks)
    if later:
        return jnp.cumsum(blocks[::-1], 0)[::-1] - blocks
    return jnp.cumsum(blocks, 0) - blocks


def on_device(queries, keys, values, out_grad):
    rows, width = queries.shape
    pairs, blocks = width // PAIR, rows // BLOCK
    factor = 1.0 / math.sqrt(DH * rows * lax.axis_size("seq"))
    states = jax.ShapeDtypeStruct((blocks, pairs * DH, PAIR), jnp.float32)
    sent = jax.ShapeDtypeStruct((pairs * DH, PAIR), jnp.bfloat16)
    part = jax.ShapeDtypeStruct((rows, width), jnp.float32)
    whole = jax.ShapeDtypeStruct((rows, width), jnp.bfloat16)
    piece = jax.ShapeDtypeStruct((out_grad.shape[0], width), jnp.bfloat16)
    heads, seqs = lax.axis_size("head"), lax.axis_size("seq")
    head = lax.axis_index("head").astype(jnp.int32).reshape(1)

    def cut_pieces(source, steps, *after):
        return call(
            functools.partial(prepare_kernel, steps, heads),
            [piece] * len(steps),
            (head, source, *after),
            1.0 if not after else 0.1,
            in_specs=[SMEM, ANY if after else HBM, *[ANY] * len(after)],
            scratch_shapes=[pltpu.SemaphoreType.DMA((len(steps),))],
        )

    (leading,) = cut_pieces(pltpu.with_memory_space_constraint(out_grad, pltpu.HBM), (2,))
    steps = (*range(3, heads), 1, 0)
    *others, own = cut_pieces(out_grad, steps, leading)
    pieces = {2: exchange(leading, "head", 2)}
    for d, x in zip(steps, others):
        pieces[d] = exchange(x, "head", d)
    pieces = [pieces[d] for d in range(1, heads)]
    block_state, block_wire = call(
        first_state_kernel, [states, sent], (keys, values, own), 0.3, in_specs=[VMEM, VMEM, ANY]
    )
    if seqs == 8:
        block_got = exchange(block_wire, "seq", 1)
        block_pair = jnp.sum(block_state, 0) + wide(block_got)
    (attended_part,) = call(
        functools.partial(forward_kernel, factor), [part], (queries, keys, values), 1.0
    )
    (queries_t,) = call(
        transpose_kernel, [jax.ShapeDtypeStruct((width, rows), jnp.bfloat16)], (queries,), 0.1
    )
    grad, grad_state, grad_wire = call(
        gather_kernel,
        [whole, states, sent],
        (head, queries_t, *pieces[1:], pieces[0], own, attended_part),
        0.3,
        in_specs=[SMEM] + [VMEM] * (heads + 1) + [ANY],
    )
    key_part, value_part = call(
        functools.partial(key_value_grad_kernel, factor), [part, part], (queries, keys, values, grad), 1.7
    )
    prefix, suffix = within(block_state, False), within(grad_state, True)
    if seqs == 8:
        me = lax.axis_index("seq")
        odd, high, lower = me & 1 != 0, me & 2 != 0, me < 4
        pair_wire = wire(block_pair)
        sends = {2: jnp.where(lower, pair_wire, grad_wire), 3: grad_wire}
        sends[1], sends[2] = lax.optimization_barrier((grad_wire, sends[2]))
        got = {d: exchange(sends[d], "seq", d) for d in (2, 3, 1)}
        other = exchange(jnp.where(lower, grad_wire, pair_wire), "seq", 2)
        got_wide = {d: wide(x) for d, x in got.items()}
        block_total = block_pair + got_wide[2]
        grad_total = jnp.sum(grad_state, 0) + got_wide[2] + got_wide[1] + got_wide[3]
        last_wire = wire(jnp.where(lower, block_total, grad_total))
        last_wire, key_part, value_part = lax.optimization_barrier((last_wire, key_part, value_part))
        last = exchange(last_wire, "seq", 4)
        gots, lasts = (block_got, got[2], got[1], got[3], other), (last,)
        flags = (
            lower,
            *(lower & odd, lower == high, ~lower & ~odd, ~lower & ~high, False),
            *(~lower & odd, False, lower & ~odd, lower & ~high, lower != high),
        )
        early, late = jnp.where(lower, prefix, suffix), jnp.where(lower, suffix, prefix)
    else:
        gots, lasts, flags = (), (), (True,)
        early = prefix + sums_along(block_state, block_wire, False)[None]
        late = suffix + sums_along(grad_state, grad_wire, True)[None]
    (query_part,) = call(functools.partial(query_grad_kernel, factor), [part], (keys, values, grad), 0.9)
    operands = (queries, keys, values, grad, attended_part, query_part, key_part, value_part)
    held = [pltpu.VMEM((rows, width), jnp.bfloat16)] * 2 + [pltpu.SemaphoreType.DMA((blocks, pairs))] * 2
    *results, late = call(
        functools.partial(early_kernel, factor),
        [whole] * 4 + [states],
        (packed(*flags), early, late, *gots, *operands),
        0.2,
        in_specs=[SMEM] + [VMEM] * (10 + len(gots)),
        out_specs=[HBM] * 4 + [VMEM],
        scratch_shapes=held,
    )
    results = call(
        functools.partial(late_kernel, factor),
        [whole] * 4,
        (packed(*flags), late, *lasts, *operands, *results),
        0.2,
        in_specs=[SMEM] + [VMEM] * (9 + len(lasts)) + [HBM] * 4,
        out_specs=[HBM] * 4,
        scratch_shapes=held,
        input_output_aliases={10 + len(lasts) + i: i for i in range(4)},
    )
    return tuple(results)


def solution(mesh):
    split = P("seq", "head")
    return jax.shard_map(
        on_device,
        mesh=mesh,
        in_specs=(split, split, split, P(("seq", "head"), None)),
        out_specs=(split, split, split, split),
        check_vma=False,
    )
```

```python
import functools
import math

import jax
import jax.numpy as jnp
from jax import lax
from jax.experimental import pallas as pl
from jax.experimental.pallas import tpu as pltpu
from jax.sharding import PartitionSpec as P

DH = 64
BLOCK = 256
PAIR = 2 * DH
VMEM = pl.BlockSpec(memory_space=pltpu.VMEM)
SMEM = pl.BlockSpec(memory_space=pltpu.SMEM)
HBM = pl.BlockSpec(memory_space=pltpu.HBM)
ANY = pl.BlockSpec(memory_space=pl.ANY)


def dot(a, b, dims):
    return lax.dot_general(a, b, ((dims[:1], dims[1:]), ((), ())), preferred_element_type=jnp.float32)


def first_half(shape):
    return lax.broadcasted_iota(jnp.int32, shape, len(shape) - 1) < DH


def split_pair(x):
    mask = first_half(x.shape)
    zero = jnp.zeros_like(x)
    return jnp.where(mask, x, zero), jnp.where(mask, zero, x)


def pair_state(a, b):
    whole = dot(a, b, (0, 0))
    return jnp.where(first_half((DH, PAIR)), whole[:DH], whole[DH:])


def spread_state(state):
    return jnp.concatenate(split_pair(state), axis=0)


def masked(scores, factor, upper):
    row = lax.broadcasted_iota(jnp.int32, scores.shape, 0)
    col = lax.broadcasted_iota(jnp.int32, scores.shape, 1)
    keep = col >= row if upper else col <= row
    return jnp.where(keep, scores * factor, 0.0).astype(jnp.bfloat16)


def pair_columns(p):
    return slice(p * PAIR, (p + 1) * PAIR)


def state_rows(p):
    return slice(p * DH, (p + 1) * DH)


def block_rows(n):
    return slice(n * BLOCK, (n + 1) * BLOCK)


def state_kernel(a_ref, b_ref, out_ref, wire_ref):
    for p in range(a_ref.shape[1] // PAIR):
        total = 0.0
        for n in range(a_ref.shape[0] // BLOCK):
            state = pair_state(a_ref[block_rows(n), pair_columns(p)], b_ref[block_rows(n), pair_columns(p)])
            out_ref[n, state_rows(p), :] = state
            total = total + state
        wire_ref[state_rows(p), :] = wire(total)


def first_state_kernel(k_ref, v_ref, _, out_ref, wire_ref):
    state_kernel(k_ref, v_ref, out_ref, wire_ref)


def cut(head_ref, g_ref, pieces, steps, count, sems):
    width, copies = pieces[0].shape[1], []
    for i, (d, piece) in enumerate(zip(steps, pieces)):
        target = receiver(head_ref[0], d, count) if d else head_ref[0]
        columns = pl.ds(pl.multiple_of(target * width, width), width)
        copies.append(pltpu.make_async_copy(g_ref.at[:, columns], piece, sems.at[i]))
    for copy in copies:
        copy.start()
    for copy in copies:
        copy.wait()


def prepare_kernel(steps, count, head_ref, g_ref, *refs):
    cut(head_ref, g_ref, refs[-1 - len(steps) : -1], steps, count, refs[-1])


def transpose_kernel(x_ref, out_ref):
    for p in range(x_ref.shape[1] // PAIR):
        out_ref[pair_columns(p), :] = x_ref[:, pair_columns(p)].T


def gather_kernel(head_ref, qt_ref, *refs):
    pieces, (_, grad_ref, out_ref, wire_ref) = refs[:-4], refs[-4:]
    rows, count = pieces[0].shape[0], len(pieces)
    for d, piece in zip((*range(2, count), 1, 0), pieces):
        source = sender(head_ref[0], d, count)
        grad_ref[pl.ds(pl.multiple_of(source * rows, rows), rows), :] = piece[...]
    for p in range(qt_ref.shape[0] // PAIR):
        total = 0.0
        for n in range(grad_ref.shape[0] // BLOCK):
            whole = dot(qt_ref[pair_columns(p), block_rows(n)], grad_ref[block_rows(n), pair_columns(p)], (1, 0))
            state = jnp.where(first_half((DH, PAIR)), whole[:DH], whole[DH:])
            out_ref[n, state_rows(p), :] = state
            total = total + state
        wire_ref[state_rows(p), :] = wire(total)


def forward_kernel(factor, q_ref, k_ref, v_ref, att_ref):
    for n in range(q_ref.shape[0] // BLOCK):
        for p in range(q_ref.shape[1] // PAIR):
            at = (block_rows(n), pair_columns(p))
            q, k, v = q_ref[at], k_ref[at], v_ref[at]
            total = 0.0
            for q_head, v_head in zip(split_pair(q), split_pair(v)):
                probs = masked(dot(q_head, k, (1, 1)), factor, False)
                total = total + dot(probs, v_head, (1, 0))
            att_ref[at] = total


def query_grad_kernel(factor, k_ref, v_ref, g_ref, dq_ref):
    for n in range(k_ref.shape[0] // BLOCK):
        for p in range(k_ref.shape[1] // PAIR):
            at = (block_rows(n), pair_columns(p))
            k, v, g = k_ref[at], v_ref[at], g_ref[at]
            total = 0.0
            for k_head, g_head in zip(split_pair(k), split_pair(g)):
                dprobs = masked(dot(g_head, v, (1, 1)), factor, False)
                total = total + dot(dprobs, k_head, (1, 0))
            dq_ref[at] = total


def key_value_grad_kernel(factor, q_ref, k_ref, v_ref, g_ref, dk_ref, dv_ref):
    for n in range(q_ref.shape[0] // BLOCK):
        for p in range(q_ref.shape[1] // PAIR):
            at = (block_rows(n), pair_columns(p))
            q, k, v, g = q_ref[at], k_ref[at], v_ref[at], g_ref[at]
            dk = dv = 0.0
            for q_head, k_head, v_head, g_head in zip(*map(split_pair, (q, k, v, g))):
                probs_t = masked(dot(k_head, q, (1, 1)), factor, True)
                dv = dv + dot(probs_t, g_head, (1, 0))
                dprobs_t = masked(dot(v_head, g, (1, 1)), factor, True)
                dk = dk + dot(dprobs_t, q_head, (1, 0))
            dk_ref[at] = dk
            dv_ref[at] = dv


def join(factor, state_of, a, b):
    copies = []
    for n in range(a[0].shape[0] // BLOCK):
        for p in range(a[0].shape[1] // PAIR):
            at = (block_rows(n), pair_columns(p))
            state = spread_state(state_of(n, state_rows(p)))
            for (x_ref, part_ref, held, out_ref, sems), side in ((a, 0), (b, 1)):
                added = factor * dot(x_ref[at], state, (1, side))
                held[at] = (part_ref[at] + added).astype(jnp.bfloat16)
                copy = pltpu.make_async_copy(held.at[at], out_ref.at[at], sems.at[n, p])
                copy.start()
                copies.append(copy)
    for copy in copies:
        copy.wait()


def join_kernel(factor, forward, flags_ref, state_of, parts, refs):
    q_ref, k_ref, v_ref, g_ref, att_part, dq_part, dk_part, dv_part = parts
    att_ref, dq_ref, dk_ref, dv_ref, a_held, b_held, a_sems, b_sems = refs
    is_forward = flags_ref[0] & 1 == int(forward)

    @pl.when(is_forward)
    def _():
        a = (q_ref, att_part, a_held, att_ref, a_sems)
        b = (g_ref, dq_part, b_held, dq_ref, b_sems)
        join(factor, state_of, a, b)

    @pl.when(jnp.logical_not(is_forward))
    def _():
        a = (k_ref, dv_part, a_held, dv_ref, a_sems)
        b = (v_ref, dk_part, b_held, dk_ref, b_sems)
        join(factor, state_of, a, b)


def early_kernel(factor, flags_ref, early_ref, late_ref, *refs):
    gots, parts, late_out_ref, rest = refs[:-17], refs[-17:-9], refs[-5], (*refs[-9:-5], *refs[-4:])

    def marked(base_ref, n, rows, first):
        state = base_ref[n, rows, :]
        for i, got_ref in enumerate(gots, first):
            state = state + jnp.where(flags_ref[0] >> i & 1 == 1, wide(got_ref[rows, :]), 0.0)
        return state

    for n in range(late_ref.shape[0]):
        for p in range(late_ref.shape[1] // DH):
            late_out_ref[n, state_rows(p), :] = marked(late_ref, n, state_rows(p), 1 + len(gots))
    join_kernel(factor, True, flags_ref, lambda n, rows: wire(marked(early_ref, n, rows, 1)), parts, rest)


def late_kernel(factor, flags_ref, late_ref, *refs):
    lasts, parts, rest = refs[:-20], refs[-20:-12], refs[-8:]

    def state_of(n, rows):
        return wire(sum((wide(last_ref[rows, :]) for last_ref in lasts), late_ref[n, rows, :]))

    join_kernel(factor, False, flags_ref, state_of, parts, rest)


def in_pairs(count):
    return count & (count - 1) == 0


def receiver(index, d, count):
    return index ^ d if in_pairs(count) else lax.rem(index + d, count)


def sender(index, d, count):
    return index ^ d if in_pairs(count) else lax.rem(index - d + count, count)


def exchange(x, axis, d):
    count = lax.axis_size(axis)
    return lax.ppermute(x, axis, [(i, i ^ d if in_pairs(count) else (i + d) % count) for i in range(count)])


def passed_along(x, axis, step):
    count = lax.axis_size(axis)
    return lax.ppermute(x, axis, [(i, i + step) for i in range(count) if 0 <= i + step < count])


def call(kernel, out_shapes, operands, microseconds, out_specs=None, in_specs=None, **options):
    return pl.pallas_call(
        kernel,
        out_shape=out_shapes,
        in_specs=in_specs or [VMEM] * len(operands),
        out_specs=out_specs or [VMEM] * len(out_shapes),
        compiler_params=pltpu.CompilerParams(vmem_limit_bytes=10 * 1024 * 1024),
        cost_estimate=pl.CostEstimate(flops=int(1.15e9 * microseconds), bytes_accessed=0, transcendentals=0),
        **options,
    )(*operands)


def wire(x):
    return x.astype(jnp.bfloat16)


def wide(x):
    return x.astype(jnp.float32)


def packed(*flags):
    return sum(jnp.asarray(flag).astype(jnp.int32) << i for i, flag in enumerate(flags)).reshape(1)


def sums_along(blocks, sent, later):
    total, found, span = jnp.sum(blocks, 0), jnp.zeros(sent.shape, jnp.float32), 1
    while span < lax.axis_size("seq"):
        got = wide(passed_along(sent, "seq", -span if later else span))
        found, total = found + got, total + got
        sent = wire(total)
        span *= 2
    return found


def within(blocks, later):
    if blocks.shape[0] == 1:
        return jnp.zeros_like(blocks)
    if later:
        return jnp.cumsum(blocks[::-1], 0)[::-1] - blocks
    return jnp.cumsum(blocks, 0) - blocks


def on_device(queries, keys, values, out_grad):
    rows, width = queries.shape
    pairs, blocks = width // PAIR, rows // BLOCK
    factor = 1.0 / math.sqrt(DH * rows * lax.axis_size("seq"))
    states = jax.ShapeDtypeStruct((blocks, pairs * DH, PAIR), jnp.float32)
    sent = jax.ShapeDtypeStruct((pairs * DH, PAIR), jnp.bfloat16)
    part = jax.ShapeDtypeStruct((rows, width), jnp.float32)
    whole = jax.ShapeDtypeStruct((rows, width), jnp.bfloat16)
    piece = jax.ShapeDtypeStruct((out_grad.shape[0], width), jnp.bfloat16)
    heads, seqs = lax.axis_size("head"), lax.axis_size("seq")
    head = lax.axis_index("head").astype(jnp.int32).reshape(1)

    def cut_pieces(source, steps, *after):
        return call(
            functools.partial(prepare_kernel, steps, heads),
            [piece] * len(steps),
            (head, source, *after),
            1.0 if not after else 0.1,
            in_specs=[SMEM, ANY if after else HBM, *[ANY] * len(after)],
            scratch_shapes=[pltpu.SemaphoreType.DMA((len(steps),))],
        )

    (leading,) = cut_pieces(pltpu.with_memory_space_constraint(out_grad, pltpu.HBM), (2,))
    steps = (*range(3, heads), 1, 0)
    *others, own = cut_pieces(out_grad, steps, leading)
    pieces = {2: exchange(leading, "head", 2)}
    for d, x in zip(steps, others):
        pieces[d] = exchange(x, "head", d)
    pieces = [pieces[d] for d in range(1, heads)]
    block_state, block_wire = call(
        first_state_kernel, [states, sent], (keys, values, own), 0.3, in_specs=[VMEM, VMEM, ANY]
    )
    if seqs == 8:
        block_got = exchange(block_wire, "seq", 1)
        block_pair = jnp.sum(block_state, 0) + wide(block_got)
    (attended_part,) = call(
        functools.partial(forward_kernel, factor), [part], (queries, keys, values), 1.0
    )
    (queries_t,) = call(
        transpose_kernel, [jax.ShapeDtypeStruct((width, rows), jnp.bfloat16)], (queries,), 0.1
    )
    grad, grad_state, grad_wire = call(
        gather_kernel,
        [whole, states, sent],
        (head, queries_t, *pieces[1:], pieces[0], own, attended_part),
        0.3,
        in_specs=[SMEM] + [VMEM] * (heads + 1) + [ANY],
    )
    key_part, value_part = call(
        functools.partial(key_value_grad_kernel, factor), [part, part], (queries, keys, values, grad), 1.7
    )
    prefix, suffix = within(block_state, False), within(grad_state, True)
    if seqs == 8:
        me = lax.axis_index("seq")
        odd, high, lower = me & 1 != 0, me & 2 != 0, me < 4
        pair_wire = wire(block_pair)
        sends = {2: jnp.where(lower, pair_wire, grad_wire), 3: grad_wire}
        sends[1], sends[2] = lax.optimization_barrier((grad_wire, sends[2]))
        got = {d: exchange(sends[d], "seq", d) for d in (2, 3, 1)}
        other = exchange(jnp.where(lower, grad_wire, pair_wire), "seq", 2)
        got_wide = {d: wide(x) for d, x in got.items()}
        block_total = block_pair + got_wide[2]
        grad_total = jnp.sum(grad_state, 0) + got_wide[2] + got_wide[1] + got_wide[3]
        last_wire = wire(jnp.where(lower, block_total, grad_total))
        last_wire, key_part, value_part = lax.optimization_barrier((last_wire, key_part, value_part))
        last = exchange(last_wire, "seq", 4)
        gots, lasts = (block_got, got[2], got[1], got[3], other), (last,)
        flags = (
            lower,
            *(lower & odd, lower == high, ~lower & ~odd, ~lower & ~high, False),
            *(~lower & odd, False, lower & ~odd, lower & ~high, lower != high),
        )
        early, late = jnp.where(lower, prefix, suffix), jnp.where(lower, suffix, prefix)
    else:
        gots, lasts, flags = (), (), (True,)
        early = prefix + sums_along(block_state, block_wire, False)[None]
        late = suffix + sums_along(grad_state, grad_wire, True)[None]
    (query_part,) = call(functools.partial(query_grad_kernel, factor), [part], (keys, values, grad), 0.9)
    operands = (queries, keys, values, grad, attended_part, query_part, key_part, value_part)
    held = [pltpu.VMEM((rows, width), jnp.bfloat16)] * 2 + [pltpu.SemaphoreType.DMA((blocks, pairs))] * 2
    *results, late = call(
        functools.partial(early_kernel, factor),
        [whole] * 4 + [states],
        (packed(*flags), early, late, *gots, *operands),
        0.2,
        in_specs=[SMEM] + [VMEM] * (10 + len(gots)),
        out_specs=[HBM] * 4 + [VMEM],
        scratch_shapes=held,
    )
    results = call(
        functools.partial(late_kernel, factor),
        [whole] * 4,
        (packed(*flags), late, *lasts, *operands, *results),
        0.2,
        in_specs=[SMEM] + [VMEM] * (9 + len(lasts)) + [HBM] * 4,
        out_specs=[HBM] * 4,
        scratch_shapes=held,
        input_output_aliases={10 + len(lasts) + i: i for i in range(4)},
    )
    return tuple(results)


def solution(mesh):
    split = P("seq", "head")
    return jax.shard_map(
        on_device,
        mesh=mesh,
        in_specs=(split, split, split, P(("seq", "head"), None)),
        out_specs=(split, split, split, split),
        check_vma=False,
    )
```

```python
import functools
import math

import jax
import jax.numpy as jnp
from jax import lax
from jax.experimental import pallas as pl
from jax.experimental.pallas import tpu as pltpu
from jax.sharding import PartitionSpec as P

DH = 64
BLOCK = 256
PAIR = 2 * DH
VMEM = pl.BlockSpec(memory_space=pltpu.VMEM)
SMEM = pl.BlockSpec(memory_space=pltpu.SMEM)
HBM = pl.BlockSpec(memory_space=pltpu.HBM)
ANY = pl.BlockSpec(memory_space=pl.ANY)


def dot(a, b, dims):
    return lax.dot_general(a, b, ((dims[:1], dims[1:]), ((), ())), preferred_element_type=jnp.float32)


def first_half(shape):
    return lax.broadcasted_iota(jnp.int32, shape, len(shape) - 1) < DH


def split_pair(x):
    mask = first_half(x.shape)
    zero = jnp.zeros_like(x)
    return jnp.where(mask, x, zero), jnp.where(mask, zero, x)


def pair_state(a, b):
    whole = dot(a, b, (0, 0))
    return jnp.where(first_half((DH, PAIR)), whole[:DH], whole[DH:])


def spread_state(state):
    return jnp.concatenate(split_pair(state), axis=0)


def masked(scores, factor, upper):
    row = lax.broadcasted_iota(jnp.int32, scores.shape, 0)
    col = lax.broadcasted_iota(jnp.int32, scores.shape, 1)
    keep = col >= row if upper else col <= row
    return jnp.where(keep, scores * factor, 0.0).astype(jnp.bfloat16)


def pair_columns(p):
    return slice(p * PAIR, (p + 1) * PAIR)


def state_rows(p):
    return slice(p * DH, (p + 1) * DH)


def block_rows(n):
    return slice(n * BLOCK, (n + 1) * BLOCK)


def state_kernel(a_ref, b_ref, out_ref, wire_ref):
    for p in range(a_ref.shape[1] // PAIR):
        total = 0.0
        for n in range(a_ref.shape[0] // BLOCK):
            state = pair_state(a_ref[block_rows(n), pair_columns(p)], b_ref[block_rows(n), pair_columns(p)])
            out_ref[n, state_rows(p), :] = state
            total = total + state
        wire_ref[state_rows(p), :] = wire(total)


def first_state_kernel(k_ref, v_ref, _, out_ref, wire_ref):
    state_kernel(k_ref, v_ref, out_ref, wire_ref)


def cut(head_ref, g_ref, pieces, steps, count, sems):
    width, copies = pieces[0].shape[1], []
    for i, (d, piece) in enumerate(zip(steps, pieces)):
        target = receiver(head_ref[0], d, count) if d else head_ref[0]
        columns = pl.ds(pl.multiple_of(target * width, width), width)
        copies.append(pltpu.make_async_copy(g_ref.at[:, columns], piece, sems.at[i]))
    for copy in copies:
        copy.start()
    for copy in copies:
        copy.wait()


def prepare_kernel(steps, count, head_ref, g_ref, *refs):
    cut(head_ref, g_ref, refs[-1 - len(steps) : -1], steps, count, refs[-1])


def transpose_kernel(x_ref, out_ref):
    for p in range(x_ref.shape[1] // PAIR):
        out_ref[pair_columns(p), :] = x_ref[:, pair_columns(p)].T


def gather_kernel(head_ref, qt_ref, *refs):
    pieces, (_, grad_ref, out_ref, wire_ref) = refs[:-4], refs[-4:]
    rows, count = pieces[0].shape[0], len(pieces)
    for d, piece in zip((*range(2, count), 1, 0), pieces):
        source = sender(head_ref[0], d, count)
        grad_ref[pl.ds(pl.multiple_of(source * rows, rows), rows), :] = piece[...]
    for p in range(qt_ref.shape[0] // PAIR):
        total = 0.0
        for n in range(grad_ref.shape[0] // BLOCK):
            whole = dot(qt_ref[pair_columns(p), block_rows(n)], grad_ref[block_rows(n), pair_columns(p)], (1, 0))
            state = jnp.where(first_half((DH, PAIR)), whole[:DH], whole[DH:])
            out_ref[n, state_rows(p), :] = state
            total = total + state
        wire_ref[state_rows(p), :] = wire(total)


def forward_kernel(factor, q_ref, k_ref, v_ref, att_ref):
    for n in range(q_ref.shape[0] // BLOCK):
        for p in range(q_ref.shape[1] // PAIR):
            at = (block_rows(n), pair_columns(p))
            q, k, v = q_ref[at], k_ref[at], v_ref[at]
            total = 0.0
            for q_head, v_head in zip(split_pair(q), split_pair(v)):
                probs = masked(dot(q_head, k, (1, 1)), factor, False)
                total = total + dot(probs, v_head, (1, 0))
            att_ref[at] = total


def query_grad_kernel(factor, k_ref, v_ref, g_ref, dq_ref):
    for n in range(k_ref.shape[0] // BLOCK):
        for p in range(k_ref.shape[1] // PAIR):
            at = (block_rows(n), pair_columns(p))
            k, v, g = k_ref[at], v_ref[at], g_ref[at]
            total = 0.0
            for k_head, g_head in zip(split_pair(k), split_pair(g)):
                dprobs = masked(dot(g_head, v, (1, 1)), factor, False)
                total = total + dot(dprobs, k_head, (1, 0))
            dq_ref[at] = total


def key_value_grad_kernel(factor, q_ref, k_ref, v_ref, g_ref, dk_ref, dv_ref):
    for n in range(q_ref.shape[0] // BLOCK):
        for p in range(q_ref.shape[1] // PAIR):
            at = (block_rows(n), pair_columns(p))
            q, k, v, g = q_ref[at], k_ref[at], v_ref[at], g_ref[at]
            dk = dv = 0.0
            for q_head, k_head, v_head, g_head in zip(*map(split_pair, (q, k, v, g))):
                probs_t = masked(dot(k_head, q, (1, 1)), factor, True)
                dv = dv + dot(probs_t, g_head, (1, 0))
                dprobs_t = masked(dot(v_head, g, (1, 1)), factor, True)
                dk = dk + dot(dprobs_t, q_head, (1, 0))
            dk_ref[at] = dk
            dv_ref[at] = dv


def join(factor, state_of, a, b):
    copies = []
    for n in range(a[0].shape[0] // BLOCK):
        for p in range(a[0].shape[1] // PAIR):
            at = (block_rows(n), pair_columns(p))
            state = spread_state(state_of(n, state_rows(p)))
            for (x_ref, part_ref, held, out_ref, sems), side in ((a, 0), (b, 1)):
                added = factor * dot(x_ref[at], state, (1, side))
                held[at] = (part_ref[at] + added).astype(jnp.bfloat16)
                copy = pltpu.make_async_copy(held.at[at], out_ref.at[at], sems.at[n, p])
                copy.start()
                copies.append(copy)
    for copy in copies:
        copy.wait()


def join_kernel(factor, forward, flags_ref, state_of, parts, refs):
    q_ref, k_ref, v_ref, g_ref, att_part, dq_part, dk_part, dv_part = parts
    att_ref, dq_ref, dk_ref, dv_ref, a_held, b_held, a_sems, b_sems = refs
    is_forward = flags_ref[0] & 1 == int(forward)

    @pl.when(is_forward)
    def _():
        a = (q_ref, att_part, a_held, att_ref, a_sems)
        b = (g_ref, dq_part, b_held, dq_ref, b_sems)
        join(factor, state_of, a, b)

    @pl.when(jnp.logical_not(is_forward))
    def _():
        a = (k_ref, dv_part, a_held, dv_ref, a_sems)
        b = (v_ref, dk_part, b_held, dk_ref, b_sems)
        join(factor, state_of, a, b)


def early_kernel(factor, flags_ref, early_ref, late_ref, *refs):
    gots, parts, late_out_ref, rest = refs[:-17], refs[-17:-9], refs[-5], (*refs[-9:-5], *refs[-4:])

    def marked(base_ref, n, rows, first):
        state = base_ref[n, rows, :]
        for i, got_ref in enumerate(gots, first):
            state = state + jnp.where(flags_ref[0] >> i & 1 == 1, wide(got_ref[rows, :]), 0.0)
        return state

    for n in range(late_ref.shape[0]):
        for p in range(late_ref.shape[1] // DH):
            late_out_ref[n, state_rows(p), :] = marked(late_ref, n, state_rows(p), 1 + len(gots))
    join_kernel(factor, True, flags_ref, lambda n, rows: wire(marked(early_ref, n, rows, 1)), parts, rest)


def late_kernel(factor, flags_ref, late_ref, *refs):
    lasts, parts, rest = refs[:-20], refs[-20:-12], refs[-8:]

    def state_of(n, rows):
        return wire(sum((wide(last_ref[rows, :]) for last_ref in lasts), late_ref[n, rows, :]))

    join_kernel(factor, False, flags_ref, state_of, parts, rest)


def in_pairs(count):
    return count & (count - 1) == 0


def receiver(index, d, count):
    return index ^ d if in_pairs(count) else lax.rem(index + d, count)


def sender(index, d, count):
    return index ^ d if in_pairs(count) else lax.rem(index - d + count, count)


def exchange(x, axis, d):
    count = lax.axis_size(axis)
    return lax.ppermute(x, axis, [(i, i ^ d if in_pairs(count) else (i + d) % count) for i in range(count)])


def passed_along(x, axis, step):
    count = lax.axis_size(axis)
    return lax.ppermute(x, axis, [(i, i + step) for i in range(count) if 0 <= i + step < count])


def call(kernel, out_shapes, operands, microseconds, out_specs=None, in_specs=None, **options):
    return pl.pallas_call(
        kernel,
        out_shape=out_shapes,
        in_specs=in_specs or [VMEM] * len(operands),
        out_specs=out_specs or [VMEM] * len(out_shapes),
        compiler_params=pltpu.CompilerParams(vmem_limit_bytes=24 * 1024 * 1024),
        cost_estimate=pl.CostEstimate(flops=int(1.15e9 * microseconds), bytes_accessed=0, transcendentals=0),
        **options,
    )(*operands)


def wire(x):
    return x.astype(jnp.bfloat16)


def wide(x):
    return x.astype(jnp.float32)


def packed(*flags):
    return sum(jnp.asarray(flag).astype(jnp.int32) << i for i, flag in enumerate(flags)).reshape(1)


def sums_along(blocks, sent, later):
    total, found, span = jnp.sum(blocks, 0), jnp.zeros(sent.shape, jnp.float32), 1
    while span < lax.axis_size("seq"):
        got = wide(passed_along(sent, "seq", -span if later else span))
        found, total = found + got, total + got
        sent = wire(total)
        span *= 2
    return found


def within(blocks, later):
    if blocks.shape[0] == 1:
        return jnp.zeros_like(blocks)
    if later:
        return jnp.cumsum(blocks[::-1], 0)[::-1] - blocks
    return jnp.cumsum(blocks, 0) - blocks


def on_device(queries, keys, values, out_grad):
    rows, width = queries.shape
    pairs, blocks = width // PAIR, rows // BLOCK
    factor = 1.0 / math.sqrt(DH * rows * lax.axis_size("seq"))
    states = jax.ShapeDtypeStruct((blocks, pairs * DH, PAIR), jnp.float32)
    sent = jax.ShapeDtypeStruct((pairs * DH, PAIR), jnp.bfloat16)
    part = jax.ShapeDtypeStruct((rows, width), jnp.float32)
    whole = jax.ShapeDtypeStruct((rows, width), jnp.bfloat16)
    piece = jax.ShapeDtypeStruct((out_grad.shape[0], width), jnp.bfloat16)
    heads, seqs = lax.axis_size("head"), lax.axis_size("seq")
    head = lax.axis_index("head").astype(jnp.int32).reshape(1)

    def cut_pieces(source, steps, *after):
        return call(
            functools.partial(prepare_kernel, steps, heads),
            [piece] * len(steps),
            (head, source, *after),
            1.0 if not after else 0.1,
            in_specs=[SMEM, ANY if after else HBM, *[ANY] * len(after)],
            scratch_shapes=[pltpu.SemaphoreType.DMA((len(steps),))],
        )

    (leading,) = cut_pieces(pltpu.with_memory_space_constraint(out_grad, pltpu.HBM), (2,))
    steps = (*range(3, heads), 1, 0)
    *others, own = cut_pieces(out_grad, steps, leading)
    pieces = {2: exchange(leading, "head", 2)}
    for d, x in zip(steps, others):
        pieces[d] = exchange(x, "head", d)
    pieces = [pieces[d] for d in range(1, heads)]
    block_state, block_wire = call(
        first_state_kernel, [states, sent], (keys, values, own), 0.3, in_specs=[VMEM, VMEM, ANY]
    )
    if seqs == 8:
        block_got = exchange(block_wire, "seq", 1)
        block_pair = jnp.sum(block_state, 0) + wide(block_got)
    (attended_part,) = call(
        functools.partial(forward_kernel, factor), [part], (queries, keys, values), 1.0
    )
    (queries_t,) = call(
        transpose_kernel, [jax.ShapeDtypeStruct((width, rows), jnp.bfloat16)], (queries,), 0.1
    )
    grad, grad_state, grad_wire = call(
        gather_kernel,
        [whole, states, sent],
        (head, queries_t, *pieces[1:], pieces[0], own, attended_part),
        0.3,
        in_specs=[SMEM] + [VMEM] * (heads + 1) + [ANY],
    )
    key_part, value_part = call(
        functools.partial(key_value_grad_kernel, factor), [part, part], (queries, keys, values, grad), 1.7
    )
    prefix, suffix = within(block_state, False), within(grad_state, True)
    if seqs == 8:
        me = lax.axis_index("seq")
        odd, high, lower = me & 1 != 0, me & 2 != 0, me < 4
        pair_wire = wire(block_pair)
        sends = {2: jnp.where(lower, pair_wire, grad_wire), 3: grad_wire}
        sends[1], sends[2] = lax.optimization_barrier((grad_wire, sends[2]))
        got = {d: exchange(sends[d], "seq", d) for d in (2, 3, 1)}
        other = exchange(jnp.where(lower, grad_wire, pair_wire), "seq", 2)
        got_wide = {d: wide(x) for d, x in got.items()}
        block_total = block_pair + got_wide[2]
        grad_total = jnp.sum(grad_state, 0) + got_wide[3] + got_wide[2] + got_wide[1]
        last_wire = wire(jnp.where(lower, block_total, grad_total))
        last_wire, key_part, value_part = lax.optimization_barrier((last_wire, key_part, value_part))
        last = exchange(last_wire, "seq", 4)
        gots, lasts = (block_got, got[3], got[2], got[1], other), (last,)
        flags = (
            lower,
            *(lower & odd, ~lower & ~high, lower == high, ~lower & ~odd, False),
            *(~lower & odd, lower & ~high, False, lower & ~odd, lower != high),
        )
        early, late = jnp.where(lower, prefix, suffix), jnp.where(lower, suffix, prefix)
    else:
        gots, lasts, flags = (), (), (True,)
        early = prefix + sums_along(block_state, block_wire, False)[None]
        late = suffix + sums_along(grad_state, grad_wire, True)[None]
    (query_part,) = call(functools.partial(query_grad_kernel, factor), [part], (keys, values, grad), 0.9)
    operands = (queries, keys, values, grad, attended_part, query_part, key_part, value_part)
    held = [pltpu.VMEM((rows, width), jnp.bfloat16)] * 2 + [pltpu.SemaphoreType.DMA((blocks, pairs))] * 2
    *results, late = call(
        functools.partial(early_kernel, factor),
        [whole] * 4 + [states],
        (packed(*flags), early, late, *gots, *operands),
        0.2,
        in_specs=[SMEM] + [VMEM] * (10 + len(gots)),
        out_specs=[HBM] * 4 + [VMEM],
        scratch_shapes=held,
    )
    results = call(
        functools.partial(late_kernel, factor),
        [whole] * 4,
        (packed(*flags), late, *lasts, *operands, *results),
        0.2,
        in_specs=[SMEM] + [VMEM] * (9 + len(lasts)) + [HBM] * 4,
        out_specs=[HBM] * 4,
        scratch_shapes=held,
        input_output_aliases={10 + len(lasts) + i: i for i in range(4)},
    )
    return tuple(results)


def solution(mesh):
    split = P("seq", "head")
    return jax.shard_map(
        on_device,
        mesh=mesh,
        in_specs=(split, split, split, P(("seq", "head"), None)),
        out_specs=(split, split, split, split),
        check_vma=False,
    )
```
